256 devices in a mesh: grp: 16 (over y, x), sub: 16 (over z, core).
Axes of the slice: x: 4, y: 4, z: 8, core: 2. Of those that a mesh axis runs over, the one named last changes fastest.
Arguments:
- loads: bfloat16 [512, 1024, 128], P(('grp', 'sub')), may hold values from -6 to 6
- schur: bfloat16 [512, 1024, 1024], P(('grp', 'sub')), may hold values from -0.5 to 3.5, as said below
- neumann: bfloat16 [512, 1024, 1024], P(('grp', 'sub')), may hold values from -0.5 to 1.5, as said below
- basis: bfloat16 [512, 24, 1024], P(('grp', 'sub')), may hold values from -0.375 to 0.375
- dof_order: int32 [512, 4, 256], P(('grp', 'sub')), may hold values from 0 to 255, each once within a row
- primal_map: int32 [512, 24], P(('grp', 'sub')), may hold values from 0 to 2047
- emitter_counts: int32 [512], replicated, may hold values from 0 to 15
- coarse_inverse: float32 [2048, 2048], P('sub'), may hold values from -0.5 to 0.5, as said below
Outputs:
- solution: float32 [512, 1024, 128], P(('grp', 'sub'))
The draws below stay inside these ranges and needn't reach their ends.
Inputs may be any that keep to these rules, and one draw needn't show every extreme that they name: `schur`: each block is symmetric positive definite. `neumann`: each block is symmetric positive definite. `coarse_inverse`: symmetric positive definite.
All inputs are finite; a program needn't handle non-finite values.
Results may differ from the reference program's by a relative error of at most 0.0022.
Values sent between devices are 32-bit elements; how exact they have to be, the bound alone decides.
No kernel may reach another device: no remote copies, remote signals or barrier semaphores. Data moves between devices by JAX's collectives and lax.ppermute only.
A program may use at most 64 MiB of HBM per device.

```python
import math
import jax
import jax.numpy as jnp
import numpy as np
from jax import lax

NI = 1024
PRIM = 24
NRHS = 128
SUB_DEV = 2
ITERS = 2
SUBS = 512
NC = 2048
N_GRP = 16
N_SUB = 16


def symmetric_block(key, leading, order, lowest, highest, spread):
    first_key, second_key = jax.random.split(key)
    noise = jax.random.normal(first_key, leading + (order, order), jnp.float32)
    mirrored = (noise + jnp.swapaxes(noise, -1, -2)) * (0.5 * spread / math.sqrt(order))
    diagonal = jax.random.uniform(second_key, leading + (order,), jnp.float32, lowest, highest)
    return mirrored + diagonal[..., None] * jnp.eye(order, dtype=jnp.float32)


def draw_schur(key, part):
    key = jax.random.fold_in(key, 11)
    return symmetric_block(key, (SUBS,), NI, 1.5, 3.0, 0.6).astype(jnp.bfloat16)


def draw_neumann(key, part):
    key = jax.random.fold_in(key, 12)
    return symmetric_block(key, (SUBS,), NI, 0.5, 1.0, 0.2).astype(jnp.bfloat16)


def draw_coarse_inverse(key, part):
    key = jax.random.fold_in(key, 13)
    return symmetric_block(key, (), NC, 0.2, 0.4, 0.1)


def set_ends(result, key, low, top_value):
    dims = result.shape
    spot = [jax.random.randint(jax.random.fold_in(key, axis), (), 0, dims[axis]) for axis in range(len(dims))]
    result = result.at[tuple(spot)].set(low)
    longest = dims.index(max(dims))
    spot[longest] = (spot[longest] + 1) % dims[longest]
    return result.at[tuple(spot)].set(top_value)


def levels(rng, shape, pieces, smallest, top_value):
    def one(axis_at, shards_of):
        steps = jax.random.uniform(jax.random.fold_in(jax.random.fold_in(rng, 6), axis_at), (shards_of,), jnp.float32, smallest / len(pieces), top_value / len(pieces))
        return jnp.repeat(jnp.exp(steps), shape[axis_at] // shards_of).reshape((-1,) + (1,) * (len(shape) - axis_at - 1))

    loudness = one(*pieces[0])
    for cut in pieces[1:]:
        loudness = loudness * one(*cut)
    return loudness


def cumulative_ranks(number_of, skew):
    weights = [(1 << 20) // math.isqrt(standing ** skew) + 1 for standing in range(1, number_of + 1)]
    deviation = 1 + sum(weights) // (1 << 30)
    return np.cumsum(np.array([max(1, weight // deviation) for weight in weights]))


def ranked_ids(stream_key, dims, count, skew):
    grid = cumulative_ranks(count, skew)
    ticket = jax.random.randint(jax.random.fold_in(stream_key, 1), dims, 0, int(grid[count - 1]))
    standing = jnp.searchsorted(jnp.asarray(grid, jnp.int32), ticket, side="right")
    return jax.random.permutation(jax.random.fold_in(stream_key, 2), count)[standing].astype(jnp.int32)


def normal_values(stream_key, shape, scale, limit, pieces=(), kind=jnp.bfloat16):
    array = jax.random.normal(stream_key, shape, jnp.float32) * scale
    if len(pieces) > 0:
        array = levels(stream_key, shape, pieces, -0.22, 0.18) * array
    return jnp.clip(array, min=-limit, max=limit).astype(kind)


def setup_inputs(seed: int = 0) -> dict:
    seeds = jax.random.split(jax.random.key(seed), 9)
    loads = normal_values(seeds[0], (SUBS, NI, NRHS), 1.0, 6.0, ((0, 256),))
    schur = draw_schur(jax.random.fold_in(seeds[8], 71), 0)
    neumann = draw_neumann(jax.random.fold_in(seeds[8], 71), 0)
    basis = normal_values(seeds[3], (SUBS, PRIM, NI), (NI // 4) ** -0.5, 0.375, ((0, 256),))
    dof_order = jax.vmap(lambda own: jax.random.permutation(own, NI // 4))(jax.random.split(seeds[4], SUBS * 4)).reshape((SUBS, 4, NI // 4)).astype(jnp.int32)
    primal_map = set_ends(jax.random.randint(seeds[5], (SUBS, PRIM), 0, NC), jax.random.fold_in(seeds[5], 1), 0, NC - 1).astype(jnp.int32)
    emitter_counts = set_ends(ranked_ids(seeds[6], (SUBS,), 16, 2), jax.random.fold_in(seeds[6], 3), 0, 15).astype(jnp.int32)
    coarse_inverse = draw_coarse_inverse(jax.random.fold_in(seeds[8], 71), 0)
    return dict(loads=loads, schur=schur, neumann=neumann, basis=basis, dof_order=dof_order, primal_map=primal_map, emitter_counts=emitter_counts, coarse_inverse=coarse_inverse)


HIGHEST = lax.Precision.HIGHEST


def face_partners(canon):
    empty_slab = jnp.zeros_like(canon[:1, :, 0])
    lower = jnp.concatenate([empty_slab, canon[:-1, :, 1]], axis=0)
    upper = jnp.concatenate([canon[1:, :, 0], empty_slab], axis=0)
    empty_chain = jnp.zeros_like(canon[:, :1, 0])
    previous = jnp.concatenate([empty_chain, canon[:, :-1, 3]], axis=1)
    following = jnp.concatenate([canon[:, 1:, 2], empty_chain], axis=1)
    return jnp.stack([lower, upper, previous, following], axis=2)


def batched(matrices, vectors):
    def single(pair):
        return jnp.dot(pair[0].astype(jnp.float32), pair[1].astype(jnp.float32), precision=HIGHEST)
    return lax.map(single, (matrices, vectors))


def reference(loads, schur, neumann, basis, dof_order, primal_map, emitter_counts, coarse_inverse):
    face = NI // 4
    chain = N_SUB * SUB_DEV
    row_index = (jnp.arange(4, dtype=jnp.int32)[None, :, None] * face + dof_order).reshape(SUBS, NI).astype(jnp.int32)
    inverse = jnp.argsort(row_index, axis=1).astype(jnp.int32)
    density = 1.0 + emitter_counts.astype(jnp.float32).reshape(N_GRP, chain)
    padded = jnp.pad(density, 1)
    own_rho = padded[1:-1, 1:-1][..., None]
    beside = jnp.stack([padded[:-2, 1:-1], padded[2:, 1:-1], padded[1:-1, :-2], padded[1:-1, 2:]], axis=-1)
    weights = jnp.where(beside > 0.0, own_rho / (own_rho + beside), 1.0).reshape(SUBS, 4)
    share = jnp.repeat(weights, face, axis=1)[:, :, None]

    def assemble(values):
        canon = jnp.take_along_axis(values, row_index[:, :, None], axis=1).reshape(N_GRP, chain, 4, face, NRHS)
        partners = face_partners(canon).reshape(SUBS, NI, NRHS)
        return values + jnp.take_along_axis(partners, inverse[:, :, None], axis=1)

    def inner(left, right):
        return jnp.sum(share * left * right, axis=(0, 1))

    def precondition(residual):
        rounded = (share * residual).astype(jnp.bfloat16)
        local = batched(neumann, rounded)
        moments = batched(basis, rounded)
        gathered = jnp.zeros((NC, NRHS), jnp.float32).at[primal_map.reshape(-1)].add(moments.reshape(SUBS * PRIM, NRHS))
        coarse = jnp.dot(coarse_inverse, gathered, precision=HIGHEST)
        picked = coarse[primal_map]
        local = local + batched(jnp.swapaxes(basis, 1, 2), picked)
        return assemble(share * local)

    residual = assemble(loads.astype(jnp.float32))
    solution = jnp.zeros((SUBS, NI, NRHS), jnp.float32)
    search = precondition(residual)
    inner_now = inner(residual, search)
    direction = search
    for iteration in range(ITERS):
        image = assemble(batched(schur, direction.astype(jnp.bfloat16)))
        step_size = inner_now / inner(direction, image)
        solution = solution + step_size * direction
        residual = residual - step_size * image
        if iteration + 1 < ITERS:
            search = precondition(residual)
            inner_next = inner(residual, search)
            direction = search + (inner_next / inner_now) * direction
            inner_now = inner_next
    return solution
```

```python
import functools

import jax
import jax.numpy as jnp
from jax import lax
from jax.experimental import pallas as pl
from jax.experimental.pallas import tpu as pltpu
from jax.sharding import PartitionSpec as P

F32 = jnp.float32
BF16 = jnp.bfloat16
AXES = ("grp", "sub")
LANES = 128
TILE = 8
FACE = 256
HI = 16
COLS = 4
GATHER = HI * COLS + TILE
VMEM_LIMIT = 40 * 1024 * 1024

NN = (((1,), (0,)), ((), ()))
NT = (((1,), (1,)), ((), ()))
TN = (((0,), (0,)), ((), ()))


def dot(left, right, dims=NN):
    return lax.dot_general(left, right, dims, preferred_element_type=F32)


def split(value):
    high = value.astype(BF16)
    return high, (value - high.astype(F32)).astype(BF16)


def wide(value):
    return jnp.concatenate(split(value), axis=1)


def fold(value):
    return value[:, :LANES] + value[:, LANES:]


def to_canon(order, value):
    return fold(dot(order, wide(value), TN))


def to_local(order, value):
    return fold(dot(order, wide(value)))


def rows(face):
    return pl.ds(face * FACE, FACE)


def call(kernel, out_shapes, *args, smem=(), cost=None):
    specs = [
        pl.BlockSpec(memory_space=pltpu.SMEM if i in smem else pltpu.VMEM)
        for i in range(len(args))
    ]
    return pl.pallas_call(
        kernel,
        out_shape=[jax.ShapeDtypeStruct(s, d) for s, d in out_shapes],
        in_specs=specs,
        out_specs=[pl.BlockSpec(memory_space=pltpu.VMEM) for _ in out_shapes],
        compiler_params=pltpu.CompilerParams(vmem_limit_bytes=VMEM_LIMIT),
    )(*args)


HALO_SHAPES = [
    ((2, FACE, LANES), F32),
    ((2, FACE, LANES), F32),
    ((FACE, LANES), F32),
    ((FACE, LANES), F32),
    ((2, FACE, LANES), F32),
]


def put_faces(send, order_ref, value_of, one_pass=False):
    up, down, after, before, inside = send

    def canon(s, f):
        order = order_ref[4 * s + f]
        if one_pass:
            return dot(order, value_of(s, f), TN)
        return to_canon(order, value_of(s, f))

    for s in range(2):
        up[s] = canon(s, 1)
        down[s] = canon(s, 0)
    after[...] = canon(1, 3)
    before[...] = canon(0, 2)
    inside[0] = canon(0, 3)
    inside[1] = canon(1, 2)


def partner(recv, s, f):
    lower, upper, previous, following, inside = recv
    if f == 0:
        return lower[s]
    if f == 1:
        return upper[s]
    if f == 2:
        return previous[...] if s == 0 else inside[0]
    return inside[1] if s == 0 else following[...]


def exchange(send):
    up, down, after, before, inside = send
    n_grp = lax.axis_size("grp")
    n_sub = lax.axis_size("sub")
    grp_up = [(i, i + 1) for i in range(n_grp - 1)]
    grp_down = [(i + 1, i) for i in range(n_grp - 1)]
    sub_up = [(i, i + 1) for i in range(n_sub - 1)]
    sub_down = [(i + 1, i) for i in range(n_sub - 1)]
    lower = lax.ppermute(up, "grp", grp_up)
    upper = lax.ppermute(down, "grp", grp_down)
    previous = lax.ppermute(after, "sub", sub_up)
    following = lax.ppermute(before, "sub", sub_down)
    return [lower, upper, previous, following, inside]


def share_of(share_ref, s, f):
    return share_ref[pl.ds(4 * s + f, 1), :]


def prepare_kernel(place, counts, dof, loads, order, share, *send):
    grp, sub = place[0], place[1]
    n_grp, n_sub = place[2], place[3]
    chain = 2 * n_sub

    def density(g, j):
        inside = (g >= 0) & (g < n_grp) & (j >= 0) & (j < chain)
        at = jnp.where(inside, g * chain + j, 0)
        return jnp.where(inside, counts[at].astype(F32) + 1.0, 0.0)

    for s in range(2):
        j = 2 * sub + s
        own = jnp.full((1, LANES), density(grp, j), F32)
        near = ((grp - 1, j), (grp + 1, j), (grp, j - 1), (grp, j + 1))
        for f, (g, k) in enumerate(near):
            beside = jnp.full((1, LANES), density(g, k), F32)
            share[pl.ds(4 * s + f, 1), :] = own / (own + beside)
    row = lax.broadcasted_iota(jnp.int32, (FACE, FACE), 0)
    for s in range(2):
        for f in range(4):
            order[4 * s + f] = (row == dof[s, pl.ds(f, 1), :]).astype(F32).astype(BF16)
    put_faces(send, order, lambda s, f: loads[s, rows(f), :], one_pass=True)


def coarse_split_kernel(place, own, other, high, low):
    core = place[1] % 2
    for half in range(2):
        at = pl.ds(half * LANES, LANES)
        value = jnp.where(core == half, own[...], other[...])
        first, second = split(value)
        high[at, :] = first
        low[at, :] = second


def put_message(message, values, index):
    flat = jnp.transpose(values)
    owners = LANES // COLS
    for c in range(COLS):
        message[pl.ds(c, owners, stride=TILE), :] = flat[c * owners : (c + 1) * owners]
    message[pl.ds(COLS, owners, stride=TILE), :] = jnp.broadcast_to(index[...], (owners, LANES))
    for c in range(COLS + 1, TILE):
        message[pl.ds(c, owners, stride=TILE), :] = jnp.zeros((owners, LANES), F32)


def get_message(message):
    owners = LANES // COLS
    flat = jnp.concatenate(
        [message[pl.ds(c, owners, stride=TILE), :] for c in range(COLS)], axis=0
    )
    return jnp.transpose(flat)


def residual_kernel(
    loads, lower, upper, previous, following, inside, order, share, neumann, basis, index,
    residual, local, message,
):
    recv = (lower, upper, previous, following, inside)
    moments = []
    for s in range(2):
        pieces = []
        for f in range(4):
            beside = dot(order[4 * s + f], partner(recv, s, f).astype(BF16))
            value = loads[s, rows(f), :].astype(F32) + beside
            residual[s, rows(f), :] = value
            pieces.append((share_of(share, s, f) * value).astype(BF16))
        rounded = jnp.concatenate(pieces, axis=0)
        local[s] = dot(neumann[s], rounded)
        moments.append(dot(basis[s], rounded))
    used = sum(m.shape[0] for m in moments)
    moments.append(jnp.zeros((LANES - used, LANES), F32))
    put_message(message, jnp.concatenate(moments, axis=0), index)


def scatter_kernel(received, gathered, lhs, hot):
    owners = received.shape[0] // TILE
    row = lax.broadcasted_iota(jnp.int32, (LANES, LANES), 0)
    total = jnp.zeros((TILE, LANES), F32)
    for d in range(owners):
        block = received[pl.ds(TILE * d, TILE), :]
        total = total + block
        at = block[COLS : COLS + 1].astype(jnp.int32)
        high = at >> 7
        low = at & (LANES - 1)
        span = pl.ds(d * LANES, LANES)
        hot[:, span] = (row == low).astype(F32).astype(BF16)
        spread = jnp.concatenate(
            [jnp.where(high == h, block, 0.0) for h in range(HI)], axis=0
        )
        first, second = split(spread)
        lhs[pl.ds(0, LANES), span] = first
        lhs[pl.ds(LANES, LANES), span] = second
    both = dot(lhs[...], hot[...], NT)
    sums = both[:LANES] + both[LANES:]
    packed = [sums[TILE * h : TILE * h + COLS] for h in range(HI)]
    packed = jnp.concatenate(packed + [total], axis=0)
    for z in range(gathered.shape[0] // GATHER):
        gathered[pl.ds(GATHER * z, GATHER), :] = packed


def coarse_kernel(gathered, high, low, slab, scalars):
    n_z = gathered.shape[0] // GATHER
    total = gathered[pl.ds(0, GATHER), :]
    for z in range(1, n_z):
        total = total + gathered[pl.ds(GATHER * z, GATHER), :]
    scalars[...] = total[HI * COLS :]
    flat = jnp.concatenate([total[COLS * h : COLS * h + COLS] for h in range(HI)], axis=1)
    first, second = split(flat)
    both = dot(jnp.concatenate([first, second], axis=0), high[...], NT)
    result = both[:COLS] + both[COLS:] + dot(first, low[...], NT)
    tile = jnp.concatenate([result[:, :LANES], result[:, LANES:]], axis=0)
    for z in range(n_z):
        slab[pl.ds(TILE * z, TILE), :] = tile


def pick_kernel(coarse, received, scalars, message):
    owners = received.shape[0] // TILE
    row = lax.broadcasted_iota(jnp.int32, (LANES, LANES), 0)
    tile_row = lax.broadcasted_iota(jnp.int32, (TILE, LANES), 0)
    lane = lax.broadcasted_iota(jnp.int32, (TILE, LANES), 1)
    first, second = split(coarse[...])
    table = jnp.concatenate([first, second], axis=0)
    extra = scalars[...]
    for d in range(owners):
        at = received[pl.ds(TILE * d + COLS, 1), :].astype(jnp.int32)
        high = at >> 7
        low = at & (LANES - 1)
        hot = (row == low).astype(F32).astype(BF16)
        both = dot(table, hot)
        value = both[: HI * COLS] + both[HI * COLS :]
        total = jnp.zeros((TILE, LANES), F32)
        for v in range(HI * COLS // TILE):
            here = high == (tile_row // COLS + 2 * v)
            total = total + jnp.where(here, value[TILE * v : TILE * v + TILE], 0.0)
        total = total + pltpu.roll(total, COLS, 0)
        message[pl.ds(TILE * d, TILE), :] = jnp.where(lane < 48, total, extra)


def spread_basis(basis, s, picked):
    prim = basis.shape[1]
    here = picked[prim * s : prim * s + prim]
    first = here.astype(BF16).astype(F32)
    second = here - first
    both = jnp.concatenate([first, second], axis=0).astype(BF16)
    twice = jnp.concatenate([basis[s].astype(F32)] * 2, axis=0).astype(BF16)
    return dot(twice, both, TN)


def search_kernel(message, local, basis, share, order, partial, *send):
    picked = get_message(message)
    for s in range(2):
        value = local[s] + spread_basis(basis, s, picked)
        for f in range(4):
            part = value[f * FACE : f * FACE + FACE]
            partial[s, rows(f), :] = share_of(share, s, f) * part
    put_faces(send, order, lambda s, f: partial[s, rows(f), :])


def direction_kernel(
    partial, lower, upper, previous, following, inside, order, share, schur, residual,
    direction, image, scalars, *send,
):
    recv = (lower, upper, previous, following, inside)
    rz = jnp.zeros((1, LANES), F32)
    curve = jnp.zeros((1, LANES), F32)
    for s in range(2):
        for f in range(4):
            value = partial[s, rows(f), :] + to_local(order[4 * s + f], partner(recv, s, f))
            direction[s, rows(f), :] = value
            weighted = share_of(share, s, f) * residual[s, rows(f), :] * value
            rz = rz + jnp.sum(weighted, axis=0, keepdims=True)
        whole = direction[s]
        product = dot(schur[s], whole.astype(BF16))
        image[s] = product
        curve = curve + jnp.sum(whole * product, axis=0, keepdims=True)
    scalars[...] = jnp.concatenate([rz, curve, jnp.zeros((TILE - 2, LANES), F32)], axis=0)
    put_faces(send, order, lambda s, f: image[s, rows(f), :])


def image_kernel(
    partial, lower, upper, previous, following, inside, order, share, basis, index, scalars,
    image, message,
):
    recv = (lower, upper, previous, following, inside)
    moments = []
    for s in range(2):
        pieces = []
        for f in range(4):
            value = partial[s, rows(f), :] + to_local(order[4 * s + f], partner(recv, s, f))
            image[s, rows(f), :] = value
            pieces.append(wide(share_of(share, s, f) * value))
        moments.append(fold(dot(basis[s], jnp.concatenate(pieces, axis=0))))
    moments.append(scalars[...])
    used = sum(m.shape[0] for m in moments)
    moments.append(jnp.zeros((LANES - used, LANES), F32))
    put_message(message, jnp.concatenate(moments, axis=0), index)


def update_kernel(
    residual, image, first_message, message, neumann, basis, share, order,
    fresh, partial, scalars, *send,
):
    picked = get_message(message)
    rz, curve = picked[48:49], picked[49:50]
    step = rz / curve
    scalars[...] = jnp.concatenate([rz, curve, step, jnp.zeros((TILE - 3, LANES), F32)], axis=0)
    coarse = get_message(first_message) - step * picked
    for s in range(2):
        pieces = []
        for f in range(4):
            value = residual[s, rows(f), :] - step * image[s, rows(f), :]
            fresh[s, rows(f), :] = value
            pieces.append((share_of(share, s, f) * value).astype(BF16))
        local = dot(neumann[s], jnp.concatenate(pieces, axis=0))
        local = local + spread_basis(basis, s, coarse)
        for f in range(4):
            part = local[f * FACE : f * FACE + FACE]
            partial[s, rows(f), :] = share_of(share, s, f) * part
    put_faces(send, order, lambda s, f: partial[s, rows(f), :])


def last_kernel(
    partial, lower, upper, previous, following, inside, order, share, schur, residual, image,
    search, message,
):
    recv = (lower, upper, previous, following, inside)
    rz = jnp.zeros((1, LANES), F32)
    same = jnp.zeros((1, LANES), F32)
    cross = jnp.zeros((1, LANES), F32)
    for s in range(2):
        for f in range(4):
            value = partial[s, rows(f), :] + to_local(order[4 * s + f], partner(recv, s, f))
            search[s, rows(f), :] = value
            weighted = share_of(share, s, f) * residual[s, rows(f), :] * value
            rz = rz + jnp.sum(weighted, axis=0, keepdims=True)
        whole = search[s]
        rounded = whole.astype(BF16)
        product = dot(schur[s], rounded)
        twice = 2.0 * whole - rounded.astype(F32)
        same = same + jnp.sum(twice * product, axis=0, keepdims=True)
        cross = cross + jnp.sum(whole * image[s], axis=0, keepdims=True)
    tile = jnp.concatenate([rz, same, cross, jnp.zeros((TILE - 3, LANES), F32)], axis=0)
    for d in range(message.shape[0] // TILE):
        message[pl.ds(TILE * d, TILE), :] = tile


def sum_tiles(received):
    total = received[pl.ds(0, TILE), :]
    for d in range(1, received.shape[0] // TILE):
        total = total + received[pl.ds(TILE * d, TILE), :]
    return total


def sum_kernel(received, out):
    total = sum_tiles(received)
    for z in range(out.shape[0] // TILE):
        out[pl.ds(TILE * z, TILE), :] = total


def finish_kernel(received, scalars, direction, search, out):
    total = sum_tiles(received)
    rz, curve, step = scalars[0:1, :], scalars[1:2, :], scalars[2:3, :]
    rz_next, same, cross = total[0:1], total[1:2], total[2:3]
    beta = rz_next / rz
    curve_next = same + 2.0 * beta * cross + beta * beta * curve
    step_next = rz_next / curve_next
    along = step + step_next * beta
    for s in range(2):
        out[s] = along * direction[s] + step_next * search[s]


def body(loads, schur, neumann, basis, dof_order, primal_map, emitter_counts, coarse_inverse):
    n_grp = lax.axis_size("grp")
    n_sub = lax.axis_size("sub")
    n_z = n_sub // 2
    grp = lax.axis_index("grp")
    sub = lax.axis_index("sub")
    place = jnp.stack([grp, sub, jnp.int32(n_grp), jnp.int32(n_sub)]).astype(jnp.int32)
    vector = ((2, 4 * FACE, LANES), F32)
    tile = ((TILE, LANES), F32)
    owners = 2 * n_grp
    message_shape = ((owners * TILE, LANES), F32)

    plane = [
        [g * n_sub + 2 * z + c for g in range(n_grp) for c in range(2)] for z in range(n_z)
    ]
    column = [
        [g * n_sub + 2 * z + c for z in range(n_z)] for g in range(n_grp) for c in range(2)
    ]

    def to_owners(value):
        return lax.all_to_all(value, AXES, 0, 0, axis_index_groups=plane, tiled=True)

    def along_z(value):
        return lax.all_to_all(value, AXES, 0, 0, axis_index_groups=column, tiled=True)

    prim = primal_map.size
    index = jnp.pad(
        primal_map.reshape(1, prim).astype(F32), ((0, 0), (0, LANES - prim)), constant_values=-1.0
    )
    swap = [(i, i ^ 1) for i in range(n_sub)]
    other = lax.ppermute(coarse_inverse, "sub", swap)
    order, share, *send = call(
        prepare_kernel,
        [((8, FACE, FACE), BF16), tile] + HALO_SHAPES,
        place, emitter_counts, dof_order, loads,
        smem=(0, 1),
    )
    recv = exchange(send)
    high, low = call(
        coarse_split_kernel,
        [((2 * LANES, coarse_inverse.shape[1]), BF16)] * 2,
        place, coarse_inverse, other,
        smem=(0,),
    )

    def coarse_solve(message, first):
        received = to_owners(message)
        if first is None:
            first = received
        (gathered,) = pl.pallas_call(
            scatter_kernel,
            out_shape=[jax.ShapeDtypeStruct((n_z * GATHER, LANES), F32)],
            in_specs=[pl.BlockSpec(memory_space=pltpu.VMEM)],
            out_specs=[pl.BlockSpec(memory_space=pltpu.VMEM)],
            scratch_shapes=[
                pltpu.VMEM((2 * LANES, owners * LANES), BF16),
                pltpu.VMEM((LANES, owners * LANES), BF16),
            ],
            compiler_params=pltpu.CompilerParams(vmem_limit_bytes=VMEM_LIMIT),
        )(received)
        gathered = along_z(gathered)
        slab, scalars = call(coarse_kernel, [((n_z * TILE, LANES), F32), tile], gathered, high, low)
        coarse = along_z(slab)
        (picked,) = call(pick_kernel, [message_shape], coarse, first, scalars)
        return to_owners(picked), first

    residual, local, message = call(
        residual_kernel,
        [vector, vector, message_shape],
        loads, *recv, order, share, neumann, basis, index,
    )
    picked_first, maps = coarse_solve(message, None)
    partial, *send = call(
        search_kernel, [vector] + HALO_SHAPES, picked_first, local, basis, share, order
    )
    recv = exchange(send)
    direction, product, sums, *send = call(
        direction_kernel,
        [vector, vector, tile] + HALO_SHAPES,
        partial, *recv, order, share, schur, residual,
    )
    recv = exchange(send)
    image, message = call(
        image_kernel,
        [vector, message_shape],
        product, *recv, order, share, basis, index, sums,
    )
    picked, _ = coarse_solve(message, maps)
    fresh, partial, scalars, *send = call(
        update_kernel,
        [vector, vector, tile] + HALO_SHAPES,
        residual, image, picked_first, picked, neumann, basis, share, order,
    )
    recv = exchange(send)
    search, message = call(
        last_kernel,
        [vector, message_shape],
        partial, *recv, order, share, schur, fresh, product,
    )
    (sums,) = call(sum_kernel, [((n_z * TILE, LANES), F32)], to_owners(message))
    (out,) = call(finish_kernel, [vector], along_z(sums), scalars, direction, search)
    return out


def solution(mesh):
    in_specs = (
        P(AXES, None, None),
        P(AXES, None, None),
        P(AXES, None, None),
        P(AXES, None, None),
        P(AXES, None, None),
        P(AXES, None),
        P(),
        P("sub", None),
    )
    return jax.shard_map(
        body, mesh=mesh, in_specs=in_specs, out_specs=P(AXES, None, None), check_vma=False
    )
```

```python
import functools

import jax
import jax.numpy as jnp
from jax import lax
from jax.experimental import pallas as pl
from jax.experimental.pallas import tpu as pltpu
from jax.sharding import PartitionSpec as P

F32 = jnp.float32
BF16 = jnp.bfloat16
AXES = ("grp", "sub")
LANES = 128
TILE = 8
FACE = 256
HI = 16
COLS = 4
GATHER = HI * COLS + TILE
SLOT = 32
SUMS = 24
ACROSS = 8
VMEM_LIMIT = 40 * 1024 * 1024

NN = (((1,), (0,)), ((), ()))
NT = (((1,), (1,)), ((), ()))
TN = (((0,), (0,)), ((), ()))


def dot(left, right, dims=NN):
    return lax.dot_general(left, right, dims, preferred_element_type=F32)


def split(value):
    high = value.astype(BF16)
    return high, (value - high.astype(F32)).astype(BF16)


def wide(value):
    return jnp.concatenate(split(value), axis=1)


def fold(value):
    return value[:, :LANES] + value[:, LANES:]


def to_canon(order, value):
    return fold(dot(order, wide(value), TN))


def to_local(order, value):
    return fold(dot(order, wide(value)))


def rows(face):
    return pl.ds(pl.multiple_of(face * FACE, FACE), FACE)


class Near:
    def __init__(self, shape, dtype=F32):
        self.shape, self.dtype = tuple(shape), dtype


class Far(Near):
    pass


class Fetched:
    def __init__(self, source, scratch, done):
        self.scratch = scratch
        parts = done.shape[0]
        if parts == 1:
            self.copies = [pltpu.make_async_copy(source, scratch, done.at[0])]
        else:
            self.copies = [
                pltpu.make_async_copy(source.at[i], scratch.at[i], done.at[i])
                for i in range(parts)
            ]
        self.waiting = set(range(parts))
        self.shape = source.shape
        for copy in self.copies:
            copy.start()

    def wait(self, parts):
        for i in sorted(self.waiting & set(parts)):
            self.copies[i].wait()
        self.waiting -= set(parts)

    def __getitem__(self, at):
        first = at[0] if isinstance(at, tuple) else at
        every = range(len(self.copies))
        one = isinstance(first, int) and len(self.copies) > 1
        self.wait([first] if one else every)
        return self.scratch[at]


def send(*results):
    for result in results:
        if isinstance(result, Stored):
            result.send()


class Stored:
    def __init__(self, target, scratch, done):
        self.scratch, self.shape, self.sent = scratch, scratch.shape, False
        self.copy = pltpu.make_async_copy(scratch, target, done.at[0])

    def __setitem__(self, at, value):
        self.scratch[at] = value

    def __getitem__(self, at):
        return self.scratch[at]

    def send(self):
        if not self.sent:
            self.copy.start()
            self.sent = True


def call(kernel, outs, *args, far=(), smem=(), loose=(), scratch=()):
    n_in, n_out = len(args), len(outs)
    far_in = list(far)
    far_out = [i for i, out in enumerate(outs) if isinstance(out, Far)]
    extra = []
    for i in far_in:
        kind = pltpu.SMEM if i in smem else pltpu.VMEM
        extra.append(kind(args[i].shape, args[i].dtype))
        parts = 2 if args[i].ndim == 3 and args[i].shape[0] == 2 else 1
        extra.append(pltpu.SemaphoreType.DMA((parts,)))
    for i in far_out:
        extra.append(pltpu.VMEM(outs[i].shape, outs[i].dtype))
        extra.append(pltpu.SemaphoreType.DMA((1,)))

    def whole(*refs):
        ins, results = list(refs[:n_in]), list(refs[n_in : n_in + n_out])
        rest = refs[n_in + n_out :]
        own, rest = rest[: len(scratch)], rest[len(scratch) :]
        for k, i in enumerate(far_in):
            ins[i] = Fetched(ins[i], rest[2 * k], rest[2 * k + 1])
        rest = rest[2 * len(far_in) :]
        for k, i in enumerate(far_out):
            results[i] = Stored(results[i], rest[2 * k], rest[2 * k + 1])
        kernel(*ins, *results, *own)
        for i in far_in:
            ins[i].wait(range(len(ins[i].copies)))
        for i in far_out:
            results[i].send()
        for i in far_out:
            results[i].copy.wait()

    operands = [
        pltpu.with_memory_space_constraint(a, pltpu.HBM) if i in far and i not in loose else a
        for i, a in enumerate(args)
    ]
    return pl.pallas_call(
        whole,
        out_shape=[
            pltpu.HBM(out.shape, out.dtype)
            if isinstance(out, Far)
            else jax.ShapeDtypeStruct(out.shape, out.dtype)
            for out in outs
        ],
        in_specs=[
            pl.BlockSpec(memory_space=pl.ANY if i in far else pltpu.VMEM)
            for i in range(n_in)
        ],
        out_specs=[
            pl.BlockSpec(memory_space=pl.ANY if i in far_out else pltpu.VMEM)
            for i in range(n_out)
        ],
        scratch_shapes=list(scratch) + extra,
        compiler_params=pltpu.CompilerParams(vmem_limit_bytes=VMEM_LIMIT),
    )(*operands)


def odd_slab():
    return lax.axis_index("grp") % 2


def odd_core():
    return lax.axis_index("sub") % 2


def halo_shapes(length, place):
    return [
        place((2, length, LANES)),
        place((2, length, LANES)),
        place((length, LANES)),
        place((length, LANES)),
        place((2, length, LANES)),
    ]


def put_order(order, dof):
    row = lax.broadcasted_iota(jnp.int32, (FACE, FACE), 0)
    for s in range(2):
        for f in range(4):
            order[4 * s + f] = (row == dof[s, pl.ds(f, 1), :]).astype(F32).astype(BF16)


def put_faces(faces, canon):
    slab, other_slab, core, other_core, inside = faces
    odd = odd_slab()
    for s in range(2):
        other_slab[s] = canon(s, odd)
    send(other_slab)
    for s in range(2):
        slab[s] = canon(s, 1 - odd)
    send(slab)
    odd = odd_core()
    other_core[...] = canon(odd, 2 + odd)
    send(other_core)
    core[...] = canon(1 - odd, 3 - odd)
    send(core)
    inside[0] = canon(0, 3)
    inside[1] = canon(1, 2)


def partner(recv, s, f, span):
    slab, other_slab, core, other_core, inside = recv
    if f < 2:
        here, there = slab[s, span, :], other_slab[s, span, :]
        return jnp.where(odd_slab() == f, there, here)
    if s != f - 2:
        return inside[1 - s, span, :]
    here, there = core[span, :], other_core[span, :]
    return jnp.where(odd_core() == 1 - s, here, there)


WHOLE = pl.ds(0, FACE)


def exchange(send):
    slab, other_slab, core, other_core, inside = send
    n_grp = lax.axis_size("grp")
    n_sub = lax.axis_size("sub")

    def pairs(count, first):
        steps = [(i, i + 1) for i in range(first, count - 1, 2)]
        return steps + [(j, i) for i, j in steps]

    other_core = lax.ppermute(other_core, "sub", pairs(n_sub, 1))
    other_slab = lax.ppermute(other_slab, "grp", pairs(n_grp, 1))
    slab = lax.ppermute(slab, "grp", pairs(n_grp, 0))
    core = lax.ppermute(core, "sub", pairs(n_sub, 0))
    return [slab, other_slab, core, other_core, inside]


def share_of(weights, s, f):
    return weights[pl.ds(4 * s + f, 1), :]


def across_of(weights, s, f):
    return weights[pl.ds(ACROSS + 4 * s + f, 1), :]


LONG = FACE + 2 * 24 + TILE


def prepare_kernel(
    dof, loads, own_basis, primal, counts,
    order, weights, weights_far, base, basis, *faces,
):
    grp, sub = lax.axis_index("grp"), lax.axis_index("sub")
    n_grp, n_sub = lax.axis_size("grp"), lax.axis_size("sub")
    chain = 2 * n_sub
    put_order(order, dof)
    index = primal[...].astype(F32)
    pad = jnp.full((1, SLOT - SUMS), -1.0, F32)
    index = jnp.concatenate(
        [index[0:1], pad, index[1:2], pad, jnp.zeros((1, LANES - 2 * SLOT), F32)], axis=1
    )
    index = jnp.broadcast_to(index, (TILE, LANES))
    loads.wait(range(2))
    own_basis.wait(range(2))

    def canon(s, f):
        at = order[4 * s + f]
        trace = dot(own_basis.scratch[s, :, rows(f)], at)
        face = dot(at, loads.scratch[s, rows(f), :], TN)
        return jnp.concatenate([face, trace[:, :LANES], trace[:, LANES:], index], axis=0)

    put_faces(faces, canon)

    def density(g, j):
        within = (g >= 0) & (g < n_grp) & (j >= 0) & (j < chain)
        at = jnp.where(within, g * chain + j, 0)
        return jnp.where(within, counts[at].astype(F32) + 1.0, 0.0)

    counts.wait([0])
    for s in range(2):
        j = 2 * sub + s
        own = jnp.full((1, LANES), density(grp, j), F32)
        near = ((grp - 1, j), (grp + 1, j), (grp, j - 1), (grp, j + 1))
        for f, (g, k) in enumerate(near):
            beside = jnp.full((1, LANES), density(g, k), F32)
            weights[pl.ds(4 * s + f, 1), :] = own / (own + beside)
            weights[pl.ds(ACROSS + 4 * s + f, 1), :] = beside / (own + beside)
    weights_far[...] = weights[...]
    base[...] = loads[...]
    for s in range(2):
        padded = [own_basis[s].astype(F32), jnp.zeros((SLOT - SUMS, 4 * FACE), F32)]
        basis[s] = jnp.concatenate(padded, axis=0).astype(BF16)


def settle_kernel(own, other, neumann, high, low, kept, done):
    copy = pltpu.make_async_copy(neumann, kept, done.at[0])
    copy.start()
    upper = odd_core() == 1
    for half in range(2):
        at = pl.ds(half * LANES, LANES)
        mine, theirs = own[...], other[...]
        value = jnp.where(upper, mine, theirs) if half else jnp.where(upper, theirs, mine)
        first, second = split(value)
        high[at, :] = first
        low[at, :] = second
    copy.wait()


def put_message(message, values, start):
    flat = jnp.transpose(values)
    owners = LANES // COLS
    for c in range(COLS):
        message[pl.ds(start + c, owners, stride=TILE), :] = flat[c * owners : (c + 1) * owners]


def get_message(message, start):
    owners = LANES // COLS
    flat = jnp.concatenate(
        [message[pl.ds(start + c, owners, stride=TILE), :] for c in range(COLS)], axis=0
    )
    return jnp.transpose(flat)


def residual_kernel(
    order, inside, other_core, other_slab, core, slab, weights, base, basis, neumann,
    local, traces, message, *faces,
):
    recv = (slab, other_slab, core, other_core, inside)
    moments = []
    scaled = []
    for s in range(2):
        pieces = []
        for f in range(4):
            at = order[4 * s + f]
            beside = dot(at, partner(recv, s, f, WHOLE).astype(BF16))
            value = base[s, rows(f), :].astype(F32) + beside
            pieces.append(wide(share_of(weights, s, f) * value))
            left = partner(recv, s, f, pl.ds(FACE, 24))
            right = partner(recv, s, f, pl.ds(FACE + 24, 24))
            trace = dot(jnp.concatenate([left, right], axis=1).astype(BF16), at, NT)
            both = [
                basis[s, :, rows(f)].astype(F32), trace, jnp.zeros((SLOT - SUMS, FACE), F32)
            ]
            traces[4 * s + f] = jnp.concatenate(both, axis=0).astype(BF16)
        scaled.append(jnp.concatenate(pieces, axis=0))
        moments.append(fold(dot(basis[s], scaled[s])))
    moments.append(jnp.zeros((LANES - 2 * SLOT, LANES), F32))
    put_message(message, jnp.concatenate(moments, axis=0), 0)
    tile = pl.ds(FACE + 48, TILE)
    own = inside[0, tile, :][0:1]
    lower = partner(recv, 0, 0, tile)[0:1]
    upper = partner(recv, 0, 1, tile)[0:1]
    previous = partner(recv, 0, 2, tile)[0:1]
    following = partner(recv, 1, 3, tile)[0:1]
    first = jnp.concatenate([own[:, : 2 * SLOT], lower[:, : 2 * SLOT]], axis=1)
    second = jnp.concatenate(
        [upper[:, : 2 * SLOT], previous[:, SLOT : 2 * SLOT], following[:, :SLOT]], axis=1
    )
    owners = LANES // COLS
    for c, line in ((COLS, first), (COLS + 1, second)):
        message[pl.ds(c, owners, stride=TILE), :] = jnp.broadcast_to(line, (owners, LANES))
    for c in range(COLS + 2, TILE):
        message[pl.ds(c, owners, stride=TILE), :] = jnp.zeros((owners, LANES), F32)
    send(traces)
    for s in range(2):
        product = fold(dot(neumann[s], scaled[s]))
        for f in range(4):
            part = product[f * FACE : f * FACE + FACE]
            local[s, rows(f), :] = share_of(weights, s, f) * part
    put_faces(faces, lambda s, f: to_canon(order[4 * s + f], local[s, rows(f), :]))


def high_low(maps, d, line):
    at = maps[pl.ds(2 * d + line, 1), :].astype(jnp.int32)
    return at >> 7, at & (LANES - 1)


def scatter(received, maps, gathered, lhs, hot, lines):
    owners = received.shape[0] // TILE
    row = lax.broadcasted_iota(jnp.int32, (LANES, LANES), 0)
    tile_row = lax.broadcasted_iota(jnp.int32, (TILE, LANES), 0)
    total = jnp.zeros((TILE, LANES), F32)
    for d in range(owners):
        block = received[pl.ds(TILE * d, TILE), :]
        total = total + block
        span = pl.ds(d * LANES, LANES)
        highs = []
        for line in range(lines):
            high, low = high_low(maps, d, line)
            highs.append(high)
            hot[pl.ds(line * LANES, LANES), span] = (row == low).astype(F32).astype(BF16)
        high = highs[0]
        if lines == 2:
            high = jnp.where(tile_row < COLS, highs[0], highs[1])
        spread = jnp.concatenate([jnp.where(high == h, block, 0.0) for h in range(HI)], axis=0)
        first, second = split(spread)
        lhs[pl.ds(0, LANES), span] = first
        lhs[pl.ds(LANES, LANES), span] = second
    both = dot(lhs[...], hot[pl.ds(0, lines * LANES), :], NT)
    both = both[:LANES] + both[LANES:]
    packed = []
    for h in range(HI):
        value = both[TILE * h : TILE * h + COLS, :LANES]
        if lines == 2:
            value = value + both[TILE * h + COLS : TILE * h + TILE, LANES:]
        packed.append(value)
    packed = jnp.concatenate(packed + [total], axis=0)
    for z in range(gathered.shape[0] // GATHER):
        gathered[pl.ds(GATHER * z, GATHER), :] = packed


def scatter_kernel(received, gathered, maps, lhs, hot):
    for d in range(received.shape[0] // TILE):
        maps[pl.ds(2 * d, 2), :] = received[pl.ds(TILE * d + COLS, 2), :]
    send(maps)
    scatter(received, maps, gathered, lhs, hot, 1)


def coarse_kernel(gathered, high, low, slab, scalars):
    n_z = gathered.shape[0] // GATHER
    total = gathered[pl.ds(0, GATHER), :]
    for z in range(1, n_z):
        total = total + gathered[pl.ds(GATHER * z, GATHER), :]
    scalars[...] = total[HI * COLS :]
    flat = jnp.concatenate([total[COLS * h : COLS * h + COLS] for h in range(HI)], axis=1)
    first, second = split(flat)
    both = dot(jnp.concatenate([first, second], axis=0), high[...], NT)
    result = both[:COLS] + both[COLS:] + dot(first, low[...], NT)
    tile = jnp.concatenate([result[:, :LANES], result[:, LANES:]], axis=0)
    for z in range(n_z):
        slab[pl.ds(TILE * z, TILE), :] = tile


def pick_kernel(coarse, maps, scalars, message):
    owners = maps.shape[0] // 2
    row = lax.broadcasted_iota(jnp.int32, (LANES, LANES), 0)
    tile_row = lax.broadcasted_iota(jnp.int32, (TILE, LANES), 0)
    lane = lax.broadcasted_iota(jnp.int32, (TILE, LANES), 1)
    carried = (lane >= SUMS) & (lane < SLOT) & (tile_row < COLS)
    first, second = split(coarse[...])
    table = jnp.concatenate([first, second], axis=0)
    extra = scalars[...]
    for d in range(owners):
        pair = [high_low(maps, d, line) for line in range(2)]
        hot = jnp.concatenate(
            [(row == low).astype(F32).astype(BF16) for _, low in pair], axis=1
        )
        both = dot(table, hot)
        both = both[: HI * COLS] + both[HI * COLS :]
        picked = []
        for line, (high, _) in enumerate(pair):
            value = both[:, line * LANES : line * LANES + LANES]
            total = jnp.zeros((TILE, LANES), F32)
            for v in range(HI * COLS // TILE):
                here = high == (tile_row // COLS + 2 * v)
                total = total + jnp.where(here, value[TILE * v : TILE * v + TILE], 0.0)
            picked.append(total + pltpu.roll(total, COLS, 0))
        value = jnp.where(tile_row < COLS, picked[0], picked[1])
        message[pl.ds(TILE * d, TILE), :] = jnp.where(carried, extra, value)


def slots(message):
    first, second = get_message(message, 0), get_message(message, COLS)
    return [v[SLOT * i : SLOT * i + SLOT] for v in (first, second) for i in range(4)]


def neighbour(s, f):
    if f < 2:
        return 2 + 2 * f + s
    if s == f - 2:
        return 6 + s
    return 1 - s


def spread(traces, weights, picked, s, f):
    both = jnp.concatenate(
        [share_of(weights, s, f) * picked[s], across_of(weights, s, f) * picked[neighbour(s, f)]], axis=0
    )
    return fold(dot(traces[4 * s + f], wide(both), TN))


def column_sum(value):
    return jnp.sum(value, axis=0, keepdims=True)


def direction_kernel(
    returned, dof, traces, weights, local, inside, other_core, other_slab, core, slab, loads,
    schur,
    direction, image, message, *rest,
):
    faces, order = rest[:5], rest[5]
    put_order(order, dof)
    recv = (slab, other_slab, core, other_core, inside)
    picked = slots(returned)
    sums = [jnp.zeros((SLOT, LANES), F32) for _ in range(8)]
    rz = jnp.zeros((1, LANES), F32)
    curve = jnp.zeros((1, LANES), F32)
    for s in range(2):
        for f in range(4):
            value = local[s, rows(f), :] + spread(traces, weights, picked, s, f)
            value = value + to_local(order[4 * s + f], partner(recv, s, f, WHOLE))
            direction[s, rows(f), :] = value
            rz = rz + column_sum(loads[s, rows(f), :].astype(F32) * value)
        whole = direction[s]
        product = fold(dot(schur[s], wide(whole)))
        image[s] = product
        curve = curve + column_sum(whole * product)
        for f in range(4):
            both = fold(dot(traces[4 * s + f], wide(product[f * FACE : f * FACE + FACE])))
            sums[s] = sums[s] + share_of(weights, s, f) * both[:SLOT]
            to = neighbour(s, f)
            sums[to] = sums[to] + across_of(weights, s, f) * both[SLOT:]
    carried = [rz, curve, jnp.zeros((SLOT - SUMS - 2, LANES), F32)]
    first = [sums[0][:SUMS]] + carried + sums[1:4]
    send(direction, image)
    put_message(message, jnp.concatenate(first, axis=0), 0)
    put_message(message, jnp.concatenate(sums[4:], axis=0), COLS)
    put_faces(faces, lambda s, f: to_canon(order[4 * s + f], image[s, rows(f), :]))


def image_kernel(
    received, maps, dof, weights, partial, inside, other_core, other_slab, core, slab, neumann,
    gathered, local, *rest,
):
    faces, (lhs, hot, order) = rest[:5], rest[5:]
    put_order(order, dof)
    recv = (slab, other_slab, core, other_core, inside)
    scatter(received, maps, gathered, lhs, hot, 2)
    for s in range(2):
        pieces = []
        for f in range(4):
            beside = to_local(order[4 * s + f], partner(recv, s, f, WHOLE))
            value = partial[s, rows(f), :] + beside
            pieces.append(wide(share_of(weights, s, f) * value))
        product = fold(dot(neumann[s], jnp.concatenate(pieces, axis=0)))
        for f in range(4):
            part = product[f * FACE : f * FACE + FACE]
            local[s, rows(f), :] = share_of(weights, s, f) * part
    put_faces(faces, lambda s, f: to_canon(order[4 * s + f], local[s, rows(f), :]))


def last_kernel(
    returned, dof, traces, weights, local, inside, other_core, other_slab, core, slab, direction,
    loads, schur, partial,
    search, scalars, message, order,
):
    put_order(order, dof)
    recv = (slab, other_slab, core, other_core, inside)
    picked = slots(returned)
    carried = picked[0][SUMS : SUMS + 2]
    rz, curve = carried[0:1], carried[1:2]
    step = rz / curve
    scalars[...] = jnp.concatenate([rz, curve, step, jnp.zeros((TILE - 3, LANES), F32)], axis=0)
    along = jnp.zeros((1, LANES), F32)
    same = jnp.zeros((1, LANES), F32)
    cross = jnp.zeros((1, LANES), F32)
    for s in range(2):
        for f in range(4):
            value = local[s, rows(f), :] + spread(traces, weights, picked, s, f)
            value = value + to_local(order[4 * s + f], partner(recv, s, f, WHOLE))
            value = direction[s, rows(f), :] - step * value
            search[s, rows(f), :] = value
            along = along + column_sum(loads[s, rows(f), :].astype(F32) * value)
        whole = search[s]
        rounded = whole.astype(BF16)
        product = dot(schur[s], rounded)
        twice = 2.0 * whole - rounded.astype(F32)
        same = same + column_sum(twice * product)
        cross = cross + column_sum(whole * partial[s])
    send(search)
    rz_next = along - step * cross
    tile = jnp.concatenate([rz_next, same, cross, jnp.zeros((TILE - 3, LANES), F32)], axis=0)
    for d in range(message.shape[0] // TILE):
        message[pl.ds(TILE * d, TILE), :] = tile


def sum_tiles(received):
    total = received[pl.ds(0, TILE), :]
    for d in range(1, received.shape[0] // TILE):
        total = total + received[pl.ds(TILE * d, TILE), :]
    return total


def sum_kernel(received, out):
    total = sum_tiles(received)
    for z in range(out.shape[0] // TILE):
        out[pl.ds(TILE * z, TILE), :] = total


def finish_kernel(received, scalars, direction, search, out):
    total = sum_tiles(received)
    rz, curve, step = scalars[0:1, :], scalars[1:2, :], scalars[2:3, :]
    rz_next, same, cross = total[0:1], total[1:2], total[2:3]
    beta = rz_next / rz
    curve_next = same + 2.0 * beta * cross + beta * beta * curve
    step_next = rz_next / curve_next
    along = step + step_next * beta
    for s in range(2):
        out[s] = along * direction[s] + step_next * search[s]


def settle(own, other, neumann):
    return pl.pallas_call(
        settle_body,
        out_shape=[
            jax.ShapeDtypeStruct((2 * LANES, own.shape[1]), BF16),
            jax.ShapeDtypeStruct((2 * LANES, own.shape[1]), BF16),
            jax.ShapeDtypeStruct(neumann.shape, BF16),
        ],
        in_specs=[pl.BlockSpec(memory_space=pl.ANY)] * 3,
        out_specs=[pl.BlockSpec(memory_space=pltpu.VMEM)] * 3,
        scratch_shapes=[
            pltpu.VMEM(own.shape, F32),
            pltpu.VMEM(own.shape, F32),
            pltpu.SemaphoreType.DMA((1,)),
            pltpu.SemaphoreType.DMA((1,)),
            pltpu.SemaphoreType.DMA((1,)),
        ],
        compiler_params=pltpu.CompilerParams(vmem_limit_bytes=VMEM_LIMIT),
    )(*[pltpu.with_memory_space_constraint(a, pltpu.HBM) for a in (own, other, neumann)])


def settle_body(own, other, neumann, high, low, kept, own_here, other_here, a, b, c):
    fetched = Fetched(own, own_here, a), Fetched(other, other_here, b)
    settle_kernel(*fetched, neumann, high, low, kept, c)


def body(loads, schur, neumann, basis, dof_order, primal_map, emitter_counts, coarse_inverse):
    n_grp = lax.axis_size("grp")
    n_sub = lax.axis_size("sub")
    n_z = n_sub // 2
    vector = Far((2, 4 * FACE, LANES))
    tile = Far((TILE, LANES))
    owners = 2 * n_grp
    message_shape = Near((owners * TILE, LANES))

    plane = [
        [g * n_sub + 2 * z + c for g in range(n_grp) for c in range(2)] for z in range(n_z)
    ]
    column = [
        [g * n_sub + 2 * z + c for z in range(n_z)] for g in range(n_grp) for c in range(2)
    ]

    def to_owners(value):
        return lax.all_to_all(value, AXES, 0, 0, axis_index_groups=plane, tiled=True)

    def along_z(value):
        return lax.all_to_all(value, AXES, 0, 0, axis_index_groups=column, tiled=True)

    swap = [(i, i ^ 1) for i in range(n_sub)]
    other = lax.ppermute(coarse_inverse, "sub", swap)
    order, weights, weights_far, base, padded, *faces = call(
        prepare_kernel,
        [
            Near((8, FACE, FACE), BF16),
            Near((2 * TILE, LANES)),
            Far((2 * TILE, LANES)),
            Near(loads.shape, BF16),
            Near((2, SLOT, 4 * FACE), BF16),
        ]
        + halo_shapes(LONG, Near),
        dof_order, loads, basis, primal_map, emitter_counts,
        far=(0, 1, 2, 3, 4), smem=(4,),
    )

    def halo(faces):
        slab, other_slab, core, other_core, inside = exchange(faces)
        return inside, other_core, other_slab, core, slab

    recv = halo(faces)
    high, low, kept = settle(coarse_inverse, other, neumann)
    one_hot = pltpu.VMEM((8, FACE, FACE), BF16)
    lists = (
        pltpu.VMEM((2 * LANES, owners * LANES), BF16),
        pltpu.VMEM((2 * LANES, owners * LANES), BF16),
    )
    gathered_shape = Near((n_z * GATHER, LANES))

    def coarse_solve(gathered, maps):
        slab, sums = call(
            coarse_kernel, [Near((n_z * TILE, LANES)), tile], along_z(gathered), high, low
        )
        (picked,) = call(
            pick_kernel, [message_shape], along_z(slab), maps, sums, far=(1, 2)
        )
        return to_owners(picked)

    local, traces, message, *faces = call(
        residual_kernel,
        [vector, Far((8, 2 * SLOT, FACE), BF16), message_shape] + halo_shapes(FACE, Far),
        order, *recv, weights, base, padded, kept,
    )
    recv = halo(faces)
    gathered, maps = call(
        scatter_kernel, [gathered_shape, Far((2 * owners, LANES))], to_owners(message),
        scratch=lists,
    )
    returned = coarse_solve(gathered, maps)
    direction, partial, message, *faces = call(
        direction_kernel,
        [vector, vector, message_shape] + halo_shapes(FACE, Far),
        returned, dof_order, traces, weights_far, local, *recv, loads, schur,
        far=range(1, 12), loose=range(6, 10), scratch=(one_hot,),
    )
    recv = halo(faces)
    gathered, local, *faces = call(
        image_kernel,
        [gathered_shape, vector] + halo_shapes(FACE, Far),
        to_owners(message), maps, dof_order, weights_far, partial, *recv, neumann,
        far=range(1, 11), loose=range(6, 10), scratch=lists + (one_hot,),
    )
    recv = halo(faces)
    returned = coarse_solve(gathered, maps)
    search, scalars, message = call(
        last_kernel,
        [vector, tile, message_shape],
        returned, dof_order, traces, weights_far, local, *recv, direction, loads, schur, partial,
        far=range(1, 14), loose=range(6, 10), scratch=(one_hot,),
    )
    (sums,) = call(sum_kernel, [Near((n_z * TILE, LANES))], to_owners(message))
    (out,) = call(
        finish_kernel, [vector], along_z(sums), scalars, direction, search, far=(1, 2, 3)
    )
    return out


def solution(mesh):
    in_specs = (
        P(AXES, None, None),
        P(AXES, None, None),
        P(AXES, None, None),
        P(AXES, None, None),
        P(AXES, None, None),
        P(AXES, None),
        P(),
        P("sub", None),
    )
    return jax.shard_map(
        body, mesh=mesh, in_specs=in_specs, out_specs=P(AXES, None, None), check_vma=False
    )
```

```python
import functools

import jax
import jax.numpy as jnp
from jax import lax
from jax.experimental import pallas as pl
from jax.experimental.pallas import tpu as pltpu
from jax.sharding import PartitionSpec as P

F32 = jnp.float32
BF16 = jnp.bfloat16
AXES = ("grp", "sub")
LANES = 128
TILE = 8
FACE = 256
HI = 16
COLS = 4
GATHER = HI * COLS + TILE
SLOT = 32
SUMS = 24
ACROSS = 8
VMEM_LIMIT = 40 * 1024 * 1024

NN = (((1,), (0,)), ((), ()))
NT = (((1,), (1,)), ((), ()))
TN = (((0,), (0,)), ((), ()))


def dot(left, right, dims=NN):
    return lax.dot_general(left, right, dims, preferred_element_type=F32)


def split(value):
    high = value.astype(BF16)
    return high, (value - high.astype(F32)).astype(BF16)


def wide(value):
    return jnp.concatenate(split(value), axis=1)


def fold(value):
    return value[:, :LANES] + value[:, LANES:]


def to_canon(order, value):
    return fold(dot(order, wide(value), TN))


def to_local(order, value):
    return fold(dot(order, wide(value)))


def rows(face):
    return pl.ds(pl.multiple_of(face * FACE, FACE), FACE)


class Near:
    def __init__(self, shape, dtype=F32):
        self.shape, self.dtype = tuple(shape), dtype


class Far(Near):
    pass


class Fetched:
    def __init__(self, source, scratch, done):
        self.scratch = scratch
        parts = done.shape[0]
        if parts == 1:
            self.copies = [pltpu.make_async_copy(source, scratch, done.at[0])]
        else:
            self.copies = [
                pltpu.make_async_copy(source.at[i], scratch.at[i], done.at[i])
                for i in range(parts)
            ]
        self.waiting = set(range(parts))
        self.shape = source.shape
        for copy in self.copies:
            copy.start()

    def wait(self, parts):
        for i in sorted(self.waiting & set(parts)):
            self.copies[i].wait()
        self.waiting -= set(parts)

    def __getitem__(self, at):
        first = at[0] if isinstance(at, tuple) else at
        every = range(len(self.copies))
        one = isinstance(first, int) and len(self.copies) > 1
        self.wait([first] if one else every)
        return self.scratch[at]


def send(result, part=None):
    if isinstance(result, Stored):
        result.send(part)


class Stored:
    def __init__(self, target, scratch, done):
        self.scratch, self.shape = scratch, scratch.shape
        parts = done.shape[0]
        if parts == 1:
            self.copies = [pltpu.make_async_copy(scratch, target, done.at[0])]
        else:
            self.copies = [
                pltpu.make_async_copy(scratch.at[i], target.at[i], done.at[i])
                for i in range(parts)
            ]
        self.left = list(range(parts))

    def __setitem__(self, at, value):
        self.scratch[at] = value

    def __getitem__(self, at):
        return self.scratch[at]

    def send(self, part=None):
        for i in list(self.left) if part is None else [part]:
            self.copies[i].start()
            self.left.remove(i)

    def wait(self):
        for copy in self.copies:
            copy.wait()


def parts_of(array):
    return 2 if len(array.shape) == 3 and array.shape[0] == 2 else 1


def call(kernel, outs, *args, far=(), smem=(), loose=(), scratch=()):
    n_in, n_out = len(args), len(outs)
    far_in = list(far)
    far_out = [i for i, out in enumerate(outs) if isinstance(out, Far)]
    extra = []
    for i in far_in:
        kind = pltpu.SMEM if i in smem else pltpu.VMEM
        extra.append(kind(args[i].shape, args[i].dtype))
        extra.append(pltpu.SemaphoreType.DMA((parts_of(args[i]),)))
    for i in far_out:
        extra.append(pltpu.VMEM(outs[i].shape, outs[i].dtype))
        extra.append(pltpu.SemaphoreType.DMA((parts_of(outs[i]),)))

    def whole(*refs):
        ins, results = list(refs[:n_in]), list(refs[n_in : n_in + n_out])
        rest = refs[n_in + n_out :]
        own, rest = rest[: len(scratch)], rest[len(scratch) :]
        for k, i in enumerate(far_in):
            ins[i] = Fetched(ins[i], rest[2 * k], rest[2 * k + 1])
        rest = rest[2 * len(far_in) :]
        for k, i in enumerate(far_out):
            results[i] = Stored(results[i], rest[2 * k], rest[2 * k + 1])
        kernel(*ins, *results, *own)
        for i in far_in:
            ins[i].wait(range(len(ins[i].copies)))
        for i in far_out:
            results[i].send()
        for i in far_out:
            results[i].wait()

    operands = [
        pltpu.with_memory_space_constraint(a, pltpu.HBM) if i in far and i not in loose else a
        for i, a in enumerate(args)
    ]
    return pl.pallas_call(
        whole,
        out_shape=[
            pltpu.HBM(out.shape, out.dtype)
            if isinstance(out, Far)
            else jax.ShapeDtypeStruct(out.shape, out.dtype)
            for out in outs
        ],
        in_specs=[
            pl.BlockSpec(memory_space=pl.ANY if i in far else pltpu.VMEM)
            for i in range(n_in)
        ],
        out_specs=[
            pl.BlockSpec(memory_space=pl.ANY if i in far_out else pltpu.VMEM)
            for i in range(n_out)
        ],
        scratch_shapes=list(scratch) + extra,
        compiler_params=pltpu.CompilerParams(vmem_limit_bytes=VMEM_LIMIT),
    )(*operands)


def odd_slab():
    return lax.axis_index("grp") % 2


def odd_core():
    return lax.axis_index("sub") % 2


def halo_shapes(length, place):
    return [
        place((2, length, LANES)),
        place((2, length, LANES)),
        place((length, LANES)),
        place((length, LANES)),
        place((2, length, LANES)),
    ]


def put_order(order, dof):
    row = lax.broadcasted_iota(jnp.int32, (FACE, FACE), 0)
    for s in range(2):
        for f in range(4):
            order[4 * s + f] = (row == dof[s, pl.ds(f, 1), :]).astype(F32).astype(BF16)


def put_slab_faces(faces, canon, s):
    slab, other_slab = faces[:2]
    odd = odd_slab()
    other_slab[s] = canon(s, odd)
    send(other_slab, s)
    slab[s] = canon(s, 1 - odd)
    send(slab, s)


def put_core_faces(faces, canon):
    core, other_core, inside = faces[2:]
    odd = odd_core()
    other_core[...] = canon(odd, 2 + odd)
    send(other_core)
    core[...] = canon(1 - odd, 3 - odd)
    send(core)
    inside[0] = canon(0, 3)
    inside[1] = canon(1, 2)
    send(inside)


def put_faces(faces, canon):
    for s in range(2):
        put_slab_faces(faces, canon, s)
    put_core_faces(faces, canon)


def partner(recv, s, f, span):
    slab, other_slab, core, other_core, inside = recv
    if f < 2:
        here, there = slab[s, span, :], other_slab[s, span, :]
        return jnp.where(odd_slab() == f, there, here)
    if s != f - 2:
        return inside[1 - s, span, :]
    here, there = core[span, :], other_core[span, :]
    return jnp.where(odd_core() == 1 - s, here, there)


WHOLE = pl.ds(0, FACE)


def exchange(send):
    slab, other_slab, core, other_core, inside = send
    n_grp = lax.axis_size("grp")
    n_sub = lax.axis_size("sub")

    def pairs(count, first):
        steps = [(i, i + 1) for i in range(first, count - 1, 2)]
        return steps + [(j, i) for i, j in steps]

    other_core = lax.ppermute(other_core, "sub", pairs(n_sub, 1))
    other_slab = lax.ppermute(other_slab, "grp", pairs(n_grp, 1))
    slab = lax.ppermute(slab, "grp", pairs(n_grp, 0))
    core = lax.ppermute(core, "sub", pairs(n_sub, 0))
    return [slab, other_slab, core, other_core, inside]


def share_of(weights, s, f):
    return weights[pl.ds(4 * s + f, 1), :]


def across_of(weights, s, f):
    return weights[pl.ds(ACROSS + 4 * s + f, 1), :]


LONG = FACE + 2 * 24 + TILE


def prepare_kernel(
    dof, loads, own_basis, primal, counts,
    order, weights, base, basis, *faces,
):
    grp, sub = lax.axis_index("grp"), lax.axis_index("sub")
    n_grp, n_sub = lax.axis_size("grp"), lax.axis_size("sub")
    chain = 2 * n_sub
    put_order(order, dof)
    index = primal[...].astype(F32)
    pad = jnp.full((1, SLOT - SUMS), -1.0, F32)
    index = jnp.concatenate(
        [index[0:1], pad, index[1:2], pad, jnp.zeros((1, LANES - 2 * SLOT), F32)], axis=1
    )
    index = jnp.broadcast_to(index, (TILE, LANES))
    loads.wait(range(2))
    own_basis.wait(range(2))

    def canon(s, f):
        at = order[4 * s + f]
        trace = dot(own_basis.scratch[s, :, rows(f)], at)
        face = dot(at, loads.scratch[s, rows(f), :], TN)
        return jnp.concatenate([face, trace[:, :LANES], trace[:, LANES:], index], axis=0)

    put_faces(faces, canon)

    def density(g, j):
        within = (g >= 0) & (g < n_grp) & (j >= 0) & (j < chain)
        at = jnp.where(within, g * chain + j, 0)
        return jnp.where(within, counts[at].astype(F32) + 1.0, 0.0)

    counts.wait([0])
    for s in range(2):
        j = 2 * sub + s
        own = jnp.full((1, LANES), density(grp, j), F32)
        near = ((grp - 1, j), (grp + 1, j), (grp, j - 1), (grp, j + 1))
        for f, (g, k) in enumerate(near):
            beside = jnp.full((1, LANES), density(g, k), F32)
            weights[pl.ds(4 * s + f, 1), :] = own / (own + beside)
            weights[pl.ds(ACROSS + 4 * s + f, 1), :] = beside / (own + beside)
    base[...] = loads[...]
    for s in range(2):
        padded = [own_basis[s].astype(F32), jnp.zeros((SLOT - SUMS, 4 * FACE), F32)]
        basis[s] = jnp.concatenate(padded, axis=0).astype(BF16)


def settle_kernel(own, other, neumann, high, low, kept, done):
    copy = pltpu.make_async_copy(neumann, kept, done.at[0])
    copy.start()
    upper = odd_core() == 1
    for half in range(2):
        at = pl.ds(half * LANES, LANES)
        mine, theirs = own[...], other[...]
        value = jnp.where(upper, mine, theirs) if half else jnp.where(upper, theirs, mine)
        first, second = split(value)
        high[at, :] = first
        low[at, :] = second
    copy.wait()


def put_message(message, values, start):
    flat = jnp.transpose(values)
    owners = LANES // COLS
    for c in range(COLS):
        message[pl.ds(start + c, owners, stride=TILE), :] = flat[c * owners : (c + 1) * owners]


def get_message(message, start):
    owners = LANES // COLS
    flat = jnp.concatenate(
        [message[pl.ds(start + c, owners, stride=TILE), :] for c in range(COLS)], axis=0
    )
    return jnp.transpose(flat)


def residual_kernel(
    order, inside, other_core, other_slab, core, slab, weights, base, basis, neumann,
    local, traces, message, *faces,
):
    recv = (slab, other_slab, core, other_core, inside)
    moments = []
    scaled = []
    for s in range(2):
        pieces = []
        for f in range(4):
            at = order[4 * s + f]
            beside = dot(at, partner(recv, s, f, WHOLE).astype(BF16))
            value = base[s, rows(f), :].astype(F32) + beside
            pieces.append((share_of(weights, s, f) * value).astype(BF16))
            left = partner(recv, s, f, pl.ds(FACE, 24))
            right = partner(recv, s, f, pl.ds(FACE + 24, 24))
            trace = dot(jnp.concatenate([left, right], axis=1).astype(BF16), at, NT)
            both = [
                basis[s, :, rows(f)].astype(F32), trace, jnp.zeros((SLOT - SUMS, FACE), F32)
            ]
            traces[4 * s + f] = jnp.concatenate(both, axis=0).astype(BF16)
        scaled.append(jnp.concatenate(pieces, axis=0))
        moments.append(dot(basis[s], scaled[s]))
    moments.append(jnp.zeros((LANES - 2 * SLOT, LANES), F32))
    put_message(message, jnp.concatenate(moments, axis=0), 0)
    tile = pl.ds(FACE + 48, TILE)
    own = inside[0, tile, :][0:1]
    lower = partner(recv, 0, 0, tile)[0:1]
    upper = partner(recv, 0, 1, tile)[0:1]
    previous = partner(recv, 0, 2, tile)[0:1]
    following = partner(recv, 1, 3, tile)[0:1]
    first = jnp.concatenate([own[:, : 2 * SLOT], lower[:, : 2 * SLOT]], axis=1)
    second = jnp.concatenate(
        [upper[:, : 2 * SLOT], previous[:, SLOT : 2 * SLOT], following[:, :SLOT]], axis=1
    )
    owners = LANES // COLS
    for c, line in ((COLS, first), (COLS + 1, second)):
        message[pl.ds(c, owners, stride=TILE), :] = jnp.broadcast_to(line, (owners, LANES))
    for c in range(COLS + 2, TILE):
        message[pl.ds(c, owners, stride=TILE), :] = jnp.zeros((owners, LANES), F32)
    send(traces)

    def canon(s, f):
        return to_canon(order[4 * s + f], local[s, rows(f), :])

    for s in range(2):
        product = dot(neumann[s], scaled[s])
        for f in range(4):
            part = product[f * FACE : f * FACE + FACE]
            local[s, rows(f), :] = share_of(weights, s, f) * part
        send(local, s)
        put_slab_faces(faces, canon, s)
    put_core_faces(faces, canon)


def high_low(maps, row):
    at = maps[pl.ds(row, 1), :].astype(jnp.int32)
    return at >> 7, at & (LANES - 1)


def scatter(received, maps, row_at, gathered, lhs, hot, lines):
    owners = received.shape[0] // TILE
    row = lax.broadcasted_iota(jnp.int32, (LANES, LANES), 0)
    tile_row = lax.broadcasted_iota(jnp.int32, (TILE, LANES), 0)
    total = jnp.zeros((TILE, LANES), F32)
    for d in range(owners):
        block = received[pl.ds(TILE * d, TILE), :]
        total = total + block
        span = pl.ds(d * LANES, LANES)
        highs = []
        for line in range(lines):
            high, low = high_low(maps, row_at(d, line))
            highs.append(high)
            hot[pl.ds(line * LANES, LANES), span] = (row == low).astype(F32).astype(BF16)
        high = highs[0]
        if lines == 2:
            high = jnp.where(tile_row < COLS, highs[0], highs[1])
        spread = jnp.concatenate([jnp.where(high == h, block, 0.0) for h in range(HI)], axis=0)
        first, second = split(spread)
        lhs[pl.ds(0, LANES), span] = first
        lhs[pl.ds(LANES, LANES), span] = second
    both = dot(lhs[...], hot[pl.ds(0, lines * LANES), :], NT)
    both = both[:LANES] + both[LANES:]
    packed = []
    for h in range(HI):
        value = both[TILE * h : TILE * h + COLS, :LANES]
        if lines == 2:
            value = value + both[TILE * h + COLS : TILE * h + TILE, LANES:]
        packed.append(value)
    packed = jnp.concatenate(packed + [total], axis=0)
    for z in range(gathered.shape[0] // GATHER):
        gathered[pl.ds(GATHER * z, GATHER), :] = packed


def scatter_kernel(received, gathered, maps, lhs, hot):
    for d in range(received.shape[0] // TILE):
        maps[pl.ds(2 * d, 2), :] = received[pl.ds(TILE * d + COLS, 2), :]
    send(maps)
    scatter(received, received, lambda d, k: TILE * d + COLS + k, gathered, lhs, hot, 1)


def coarse_kernel(gathered, high, low, slab, scalars):
    n_z = gathered.shape[0] // GATHER
    total = gathered[pl.ds(0, GATHER), :]
    for z in range(1, n_z):
        total = total + gathered[pl.ds(GATHER * z, GATHER), :]
    scalars[...] = total[HI * COLS :]
    flat = jnp.concatenate([total[COLS * h : COLS * h + COLS] for h in range(HI)], axis=1)
    first, second = split(flat)
    both = dot(jnp.concatenate([first, second], axis=0), high[...], NT)
    result = both[:COLS] + both[COLS:] + dot(first, low[...], NT)
    tile = jnp.concatenate([result[:, :LANES], result[:, LANES:]], axis=0)
    for z in range(n_z):
        slab[pl.ds(TILE * z, TILE), :] = tile


def pick_kernel(coarse, maps, scalars, message):
    owners = maps.shape[0] // 2
    row = lax.broadcasted_iota(jnp.int32, (LANES, LANES), 0)
    tile_row = lax.broadcasted_iota(jnp.int32, (TILE, LANES), 0)
    lane = lax.broadcasted_iota(jnp.int32, (TILE, LANES), 1)
    carried = (lane >= SUMS) & (lane < SLOT) & (tile_row < COLS)
    first, second = split(coarse[...])
    table = jnp.concatenate([first, second], axis=0)
    extra = scalars[...]
    for d in range(owners):
        pair = [high_low(maps, 2 * d + line) for line in range(2)]
        hot = jnp.concatenate(
            [(row == low).astype(F32).astype(BF16) for _, low in pair], axis=1
        )
        both = dot(table, hot)
        both = both[: HI * COLS] + both[HI * COLS :]
        picked = []
        for line, (high, _) in enumerate(pair):
            value = both[:, line * LANES : line * LANES + LANES]
            total = jnp.zeros((TILE, LANES), F32)
            for v in range(HI * COLS // TILE):
                here = high == (tile_row // COLS + 2 * v)
                total = total + jnp.where(here, value[TILE * v : TILE * v + TILE], 0.0)
            picked.append(total + pltpu.roll(total, COLS, 0))
        value = jnp.where(tile_row < COLS, picked[0], picked[1])
        message[pl.ds(TILE * d, TILE), :] = jnp.where(carried, extra, value)


def slots(message):
    first, second = get_message(message, 0), get_message(message, COLS)
    return [v[SLOT * i : SLOT * i + SLOT] for v in (first, second) for i in range(4)]


def neighbour(s, f):
    if f < 2:
        return 2 + 2 * f + s
    if s == f - 2:
        return 6 + s
    return 1 - s


def spread(traces, weights, picked, s, f):
    both = jnp.concatenate(
        [share_of(weights, s, f) * picked[s], across_of(weights, s, f) * picked[neighbour(s, f)]], axis=0
    )
    return fold(dot(traces[4 * s + f], wide(both), TN))


def column_sum(value):
    return jnp.sum(value, axis=0, keepdims=True)


def direction_kernel(
    returned, dof, traces, weights, local, inside, other_core, other_slab, core, slab, loads,
    schur,
    direction, image, message, *rest,
):
    faces, order = rest[:5], rest[5]
    put_order(order, dof)
    recv = (slab, other_slab, core, other_core, inside)
    picked = slots(returned)
    sums = [jnp.zeros((SLOT, LANES), F32) for _ in range(8)]
    rz = jnp.zeros((1, LANES), F32)
    curve = jnp.zeros((1, LANES), F32)

    def canon(s, f):
        return to_canon(order[4 * s + f], image[s, rows(f), :])

    for s in range(2):
        for f in range(4):
            value = local[s, rows(f), :] + spread(traces, weights, picked, s, f)
            value = value + to_local(order[4 * s + f], partner(recv, s, f, WHOLE))
            direction[s, rows(f), :] = value
            rz = rz + column_sum(loads[s, rows(f), :].astype(F32) * value)
        whole = direction[s]
        product = dot(schur[s], whole.astype(BF16))
        image[s] = product
        curve = curve + column_sum(whole * product)
        send(direction, s)
        send(image, s)
        put_slab_faces(faces, canon, s)
    put_core_faces(faces, canon)
    for s in range(2):
        for f in range(4):
            both = fold(dot(traces[4 * s + f], wide(image[s, rows(f), :])))
            sums[s] = sums[s] + share_of(weights, s, f) * both[:SLOT]
            to = neighbour(s, f)
            sums[to] = sums[to] + across_of(weights, s, f) * both[SLOT:]
    carried = [rz, curve, jnp.zeros((SLOT - SUMS - 2, LANES), F32)]
    first = [sums[0][:SUMS]] + carried + sums[1:4]
    put_message(message, jnp.concatenate(first, axis=0), 0)
    put_message(message, jnp.concatenate(sums[4:], axis=0), COLS)


def image_kernel(
    received, maps, dof, weights, partial, inside, other_core, other_slab, core, slab, neumann,
    gathered, local, *rest,
):
    faces, (lhs, hot, order) = rest[:5], rest[5:]
    put_order(order, dof)
    recv = (slab, other_slab, core, other_core, inside)
    scatter(received, maps, lambda d, k: 2 * d + k, gathered, lhs, hot, 2)

    def canon(s, f):
        return to_canon(order[4 * s + f], local[s, rows(f), :])

    for s in range(2):
        pieces = []
        for f in range(4):
            beside = to_local(order[4 * s + f], partner(recv, s, f, WHOLE))
            value = partial[s, rows(f), :] + beside
            pieces.append(wide(share_of(weights, s, f) * value))
        product = fold(dot(neumann[s], jnp.concatenate(pieces, axis=0)))
        for f in range(4):
            part = product[f * FACE : f * FACE + FACE]
            local[s, rows(f), :] = share_of(weights, s, f) * part
        send(local, s)
        put_slab_faces(faces, canon, s)
    put_core_faces(faces, canon)


def last_kernel(
    returned, dof, traces, weights, local, inside, other_core, other_slab, core, slab, direction,
    loads, schur,
    search, scalars, message, order,
):
    put_order(order, dof)
    recv = (slab, other_slab, core, other_core, inside)
    picked = slots(returned)
    carried = picked[0][SUMS : SUMS + 2]
    rz, curve = carried[0:1], carried[1:2]
    step = rz / curve
    scalars[...] = jnp.concatenate([rz, curve, step, jnp.zeros((TILE - 3, LANES), F32)], axis=0)
    along = jnp.zeros((1, LANES), F32)
    same = jnp.zeros((1, LANES), F32)
    cross = jnp.zeros((1, LANES), F32)
    for s in range(2):
        for f in range(4):
            value = local[s, rows(f), :] + spread(traces, weights, picked, s, f)
            value = value + to_local(order[4 * s + f], partner(recv, s, f, WHOLE))
            value = direction[s, rows(f), :] - step * value
            search[s, rows(f), :] = value
            along = along + column_sum(loads[s, rows(f), :].astype(F32) * value)
        whole = search[s]
        send(search, s)
        rounded = whole.astype(BF16)
        product = dot(schur[s], rounded)
        twice = 2.0 * whole - rounded.astype(F32)
        same = same + column_sum(twice * product)
        cross = cross + column_sum(direction[s] * product)
    rz_next = along - step * cross
    tile = jnp.concatenate([rz_next, same, cross, jnp.zeros((TILE - 3, LANES), F32)], axis=0)
    for d in range(message.shape[0] // TILE):
        message[pl.ds(TILE * d, TILE), :] = tile


def sum_tiles(received):
    total = received[pl.ds(0, TILE), :]
    for d in range(1, received.shape[0] // TILE):
        total = total + received[pl.ds(TILE * d, TILE), :]
    return total


def sum_kernel(received, out):
    total = sum_tiles(received)
    for z in range(out.shape[0] // TILE):
        out[pl.ds(TILE * z, TILE), :] = total


def finish_kernel(received, scalars, direction, search, out):
    total = sum_tiles(received)
    rz, curve, step = scalars[0:1, :], scalars[1:2, :], scalars[2:3, :]
    rz_next, same, cross = total[0:1], total[1:2], total[2:3]
    beta = rz_next / rz
    curve_next = same + 2.0 * beta * cross + beta * beta * curve
    step_next = rz_next / curve_next
    along = step + step_next * beta
    for s in range(2):
        out[s] = along * direction[s] + step_next * search[s]
        send(out, s)


def settle(own, other, neumann):
    return pl.pallas_call(
        settle_body,
        out_shape=[
            jax.ShapeDtypeStruct((2 * LANES, own.shape[1]), BF16),
            jax.ShapeDtypeStruct((2 * LANES, own.shape[1]), BF16),
            jax.ShapeDtypeStruct(neumann.shape, BF16),
        ],
        in_specs=[pl.BlockSpec(memory_space=pl.ANY)] * 3,
        out_specs=[pl.BlockSpec(memory_space=pltpu.VMEM)] * 3,
        scratch_shapes=[
            pltpu.VMEM(own.shape, F32),
            pltpu.VMEM(own.shape, F32),
            pltpu.SemaphoreType.DMA((1,)),
            pltpu.SemaphoreType.DMA((1,)),
            pltpu.SemaphoreType.DMA((1,)),
        ],
        compiler_params=pltpu.CompilerParams(vmem_limit_bytes=VMEM_LIMIT),
    )(
        pltpu.with_memory_space_constraint(own, pltpu.HBM),
        other,
        pltpu.with_memory_space_constraint(neumann, pltpu.HBM),
    )


def settle_body(own, other, neumann, high, low, kept, own_here, other_here, a, b, c):
    fetched = Fetched(own, own_here, a), Fetched(other, other_here, b)
    settle_kernel(*fetched, neumann, high, low, kept, c)


def body(loads, schur, neumann, basis, dof_order, primal_map, emitter_counts, coarse_inverse):
    n_grp = lax.axis_size("grp")
    n_sub = lax.axis_size("sub")
    n_z = n_sub // 2
    vector = Far((2, 4 * FACE, LANES))
    small = Near((TILE, LANES))
    owners = 2 * n_grp
    message_shape = Near((owners * TILE, LANES))

    plane = [
        [g * n_sub + 2 * z + c for g in range(n_grp) for c in range(2)] for z in range(n_z)
    ]
    column = [
        [g * n_sub + 2 * z + c for z in range(n_z)] for g in range(n_grp) for c in range(2)
    ]

    def to_owners(value):
        return lax.all_to_all(value, AXES, 0, 0, axis_index_groups=plane, tiled=True)

    def along_z(value):
        return lax.all_to_all(value, AXES, 0, 0, axis_index_groups=column, tiled=True)

    swap = [(i, i ^ 1) for i in range(n_sub)]
    other = lax.ppermute(coarse_inverse, "sub", swap)
    order, weights, base, padded, *faces = call(
        prepare_kernel,
        [
            Near((8, FACE, FACE), BF16),
            Near((2 * TILE, LANES)),
            Near(loads.shape, BF16),
            Near((2, SLOT, 4 * FACE), BF16),
        ]
        + halo_shapes(LONG, Near),
        dof_order, loads, basis, primal_map, emitter_counts,
        far=(0, 1, 2, 3, 4), smem=(4,),
    )

    def halo(faces):
        slab, other_slab, core, other_core, inside = exchange(faces)
        return inside, other_core, other_slab, core, slab

    recv = halo(faces)
    high, low, kept = settle(coarse_inverse, other, neumann)
    one_hot = pltpu.VMEM((8, FACE, FACE), BF16)
    lists = (
        pltpu.VMEM((2 * LANES, owners * LANES), BF16),
        pltpu.VMEM((2 * LANES, owners * LANES), BF16),
    )
    gathered_shape = Near((n_z * GATHER, LANES))

    def coarse_solve(gathered, maps):
        slab, sums = call(
            coarse_kernel, [Near((n_z * TILE, LANES)), small], along_z(gathered), high, low
        )
        (picked,) = call(
            pick_kernel, [message_shape], along_z(slab), maps, sums
        )
        return to_owners(picked)

    local, traces, message, *faces = call(
        residual_kernel,
        [vector, Near((8, 2 * SLOT, FACE), BF16), message_shape] + halo_shapes(FACE, Far),
        order, *recv, weights, base, padded, kept,
    )
    recv = halo(faces)
    gathered, maps = call(
        scatter_kernel, [gathered_shape, Near((2 * owners, LANES))], to_owners(message),
        scratch=lists,
    )
    returned = coarse_solve(gathered, maps)
    direction, partial, message, *faces = call(
        direction_kernel,
        [vector, vector, message_shape] + halo_shapes(FACE, Far),
        returned, dof_order, traces, weights, local, *recv, loads, schur,
        far=[1] + list(range(4, 12)), loose=range(6, 10), scratch=(one_hot,),
    )
    recv = halo(faces)
    gathered, local, *faces = call(
        image_kernel,
        [gathered_shape, vector] + halo_shapes(FACE, Far),
        to_owners(message), maps, dof_order, weights, partial, *recv, neumann,
        far=[2] + list(range(4, 11)), loose=range(6, 10), scratch=lists + (one_hot,),
    )
    recv = halo(faces)
    returned = coarse_solve(gathered, maps)
    search, scalars, message = call(
        last_kernel,
        [vector, small, message_shape],
        returned, dof_order, traces, weights, local, *recv, direction, loads, schur,
        far=[1] + list(range(4, 13)), loose=range(6, 10), scratch=(one_hot,),
    )
    (sums,) = call(sum_kernel, [Near((n_z * TILE, LANES))], to_owners(message))
    (out,) = call(
        finish_kernel, [vector], along_z(sums), scalars, direction, search, far=(2, 3)
    )
    return out


def solution(mesh):
    in_specs = (
        P(AXES, None, None),
        P(AXES, None, None),
        P(AXES, None, None),
        P(AXES, None, None),
        P(AXES, None, None),
        P(AXES, None),
        P(),
        P("sub", None),
    )
    return jax.shard_map(
        body, mesh=mesh, in_specs=in_specs, out_specs=P(AXES, None, None), check_vma=False
    )
```

```python
import functools

import jax
import jax.numpy as jnp
from jax import lax
from jax.experimental import pallas as pl
from jax.experimental.pallas import tpu as pltpu
from jax.sharding import PartitionSpec as P

F32 = jnp.float32
BF16 = jnp.bfloat16
AXES = ("grp", "sub")
LANES = 128
TILE = 8
FACE = 256
HI = 16
COLS = 4
GATHER = HI * COLS + TILE
SLOT = 32
SUMS = 24
ACROSS = 8
VMEM_LIMIT = 40 * 1024 * 1024

NN = (((1,), (0,)), ((), ()))
NT = (((1,), (1,)), ((), ()))
TN = (((0,), (0,)), ((), ()))


def dot(left, right, dims=NN):
    return lax.dot_general(left, right, dims, preferred_element_type=F32)


def split(value):
    high = value.astype(BF16)
    return high, (value - high.astype(F32)).astype(BF16)


def wide(value):
    return jnp.concatenate(split(value), axis=1)


def fold(value):
    return value[:, :LANES] + value[:, LANES:]


def to_canon(order, value):
    return fold(dot(order, wide(value), TN))


def to_local(order, value):
    return fold(dot(order, wide(value)))


def rows(face):
    return pl.ds(pl.multiple_of(face * FACE, FACE), FACE)


class Near:
    def __init__(self, shape, dtype=F32):
        self.shape, self.dtype = tuple(shape), dtype


class Far(Near):
    pass


class Fetched:
    def __init__(self, source, scratch, done):
        self.scratch = scratch
        parts = done.shape[0]
        if parts == 1:
            self.copies = [pltpu.make_async_copy(source, scratch, done.at[0])]
        else:
            self.copies = [
                pltpu.make_async_copy(source.at[i], scratch.at[i], done.at[i])
                for i in range(parts)
            ]
        self.waiting = set(range(parts))
        self.shape = source.shape
        for copy in self.copies:
            copy.start()

    def wait(self, parts):
        for i in sorted(self.waiting & set(parts)):
            self.copies[i].wait()
        self.waiting -= set(parts)

    def __getitem__(self, at):
        first = at[0] if isinstance(at, tuple) else at
        every = range(len(self.copies))
        one = isinstance(first, int) and len(self.copies) > 1
        self.wait([first] if one else every)
        return self.scratch[at]


def send(result, part=None):
    if isinstance(result, Stored):
        result.send(part)


class Stored:
    def __init__(self, target, scratch, done):
        self.scratch, self.shape = scratch, scratch.shape
        parts = done.shape[0]
        if parts == 1:
            self.copies = [pltpu.make_async_copy(scratch, target, done.at[0])]
        else:
            self.copies = [
                pltpu.make_async_copy(scratch.at[i], target.at[i], done.at[i])
                for i in range(parts)
            ]
        self.left = list(range(parts))

    def __setitem__(self, at, value):
        self.scratch[at] = value

    def __getitem__(self, at):
        return self.scratch[at]

    def send(self, part=None):
        for i in list(self.left) if part is None else [part]:
            self.copies[i].start()
            self.left.remove(i)

    def wait(self):
        for copy in self.copies:
            copy.wait()


def parts_of(array):
    return 2 if len(array.shape) == 3 and array.shape[0] == 2 else 1


def call(kernel, outs, *args, far=(), smem=(), loose=(), scratch=()):
    n_in, n_out = len(args), len(outs)
    far_in = list(far)
    far_out = [i for i, out in enumerate(outs) if isinstance(out, Far)]
    extra = []
    for i in far_in:
        kind = pltpu.SMEM if i in smem else pltpu.VMEM
        extra.append(kind(args[i].shape, args[i].dtype))
        extra.append(pltpu.SemaphoreType.DMA((parts_of(args[i]),)))
    for i in far_out:
        extra.append(pltpu.VMEM(outs[i].shape, outs[i].dtype))
        extra.append(pltpu.SemaphoreType.DMA((parts_of(outs[i]),)))

    def whole(*refs):
        ins, results = list(refs[:n_in]), list(refs[n_in : n_in + n_out])
        rest = refs[n_in + n_out :]
        own, rest = rest[: len(scratch)], rest[len(scratch) :]
        for k, i in enumerate(far_in):
            ins[i] = Fetched(ins[i], rest[2 * k], rest[2 * k + 1])
        rest = rest[2 * len(far_in) :]
        for k, i in enumerate(far_out):
            results[i] = Stored(results[i], rest[2 * k], rest[2 * k + 1])
        kernel(*ins, *results, *own)
        for i in far_in:
            ins[i].wait(range(len(ins[i].copies)))
        for i in far_out:
            results[i].send()
        for i in far_out:
            results[i].wait()

    operands = [
        pltpu.with_memory_space_constraint(a, pltpu.HBM) if i in far and i not in loose else a
        for i, a in enumerate(args)
    ]
    return pl.pallas_call(
        whole,
        out_shape=[
            pltpu.HBM(out.shape, out.dtype)
            if isinstance(out, Far)
            else jax.ShapeDtypeStruct(out.shape, out.dtype)
            for out in outs
        ],
        in_specs=[
            pl.BlockSpec(memory_space=pl.ANY if i in far else pltpu.VMEM)
            for i in range(n_in)
        ],
        out_specs=[
            pl.BlockSpec(memory_space=pl.ANY if i in far_out else pltpu.VMEM)
            for i in range(n_out)
        ],
        scratch_shapes=list(scratch) + extra,
        compiler_params=pltpu.CompilerParams(vmem_limit_bytes=VMEM_LIMIT),
    )(*operands)


def odd_slab():
    return lax.axis_index("grp") % 2


def odd_core():
    return lax.axis_index("sub") % 2


def halo_shapes(length, place):
    return [
        place((2, length, LANES)),
        place((2, length, LANES)),
        place((length, LANES)),
        place((length, LANES)),
        place((2, length, LANES)),
    ]


def put_order(order, dof):
    row = lax.broadcasted_iota(jnp.int32, (FACE, FACE), 0)
    for s in range(2):
        for f in range(4):
            order[4 * s + f] = (row == dof[s, pl.ds(f, 1), :]).astype(F32).astype(BF16)


def put_slab_faces(faces, canon, s):
    slab, other_slab = faces[:2]
    odd = odd_slab()
    other_slab[s] = canon(s, odd)
    send(other_slab, s)
    slab[s] = canon(s, 1 - odd)
    send(slab, s)


def put_core_faces(faces, canon):
    core, other_core, inside = faces[2:]
    odd = odd_core()
    other_core[...] = canon(odd, 2 + odd)
    send(other_core)
    core[...] = canon(1 - odd, 3 - odd)
    send(core)
    inside[0] = canon(0, 3)
    inside[1] = canon(1, 2)
    send(inside)


def put_faces(faces, canon):
    for s in range(2):
        put_slab_faces(faces, canon, s)
    put_core_faces(faces, canon)


def partner(recv, s, f, span):
    slab, other_slab, core, other_core, inside = recv
    if f < 2:
        here, there = slab[s, span, :], other_slab[s, span, :]
        return jnp.where(odd_slab() == f, there, here)
    if s != f - 2:
        return inside[1 - s, span, :]
    here, there = core[span, :], other_core[span, :]
    return jnp.where(odd_core() == 1 - s, here, there)


WHOLE = pl.ds(0, FACE)


def exchange(send):
    slab, other_slab, core, other_core, inside = send
    n_grp = lax.axis_size("grp")
    n_sub = lax.axis_size("sub")

    def pairs(count, first):
        steps = [(i, i + 1) for i in range(first, count - 1, 2)]
        return steps + [(j, i) for i, j in steps]

    other_core = lax.ppermute(other_core, "sub", pairs(n_sub, 1))
    other_slab = lax.ppermute(other_slab, "grp", pairs(n_grp, 1))
    slab = lax.ppermute(slab, "grp", pairs(n_grp, 0))
    core = lax.ppermute(core, "sub", pairs(n_sub, 0))
    return [slab, other_slab, core, other_core, inside]


def share_of(weights, s, f):
    return weights[pl.ds(4 * s + f, 1), :]


def across_of(weights, s, f):
    return weights[pl.ds(ACROSS + 4 * s + f, 1), :]


LONG = FACE + 2 * 24 + TILE


def prepare_kernel(
    dof, loads, own_basis, primal, counts,
    order, weights, base, basis, *faces,
):
    grp, sub = lax.axis_index("grp"), lax.axis_index("sub")
    n_grp, n_sub = lax.axis_size("grp"), lax.axis_size("sub")
    chain = 2 * n_sub
    put_order(order, dof)
    index = primal[...].astype(F32)
    pad = jnp.full((1, SLOT - SUMS), -1.0, F32)
    index = jnp.concatenate(
        [index[0:1], pad, index[1:2], pad, jnp.zeros((1, LANES - 2 * SLOT), F32)], axis=1
    )
    index = jnp.broadcast_to(index, (TILE, LANES))
    loads.wait(range(2))
    own_basis.wait(range(2))

    def canon(s, f):
        at = order[4 * s + f]
        trace = dot(own_basis.scratch[s, :, rows(f)], at)
        face = dot(at, loads.scratch[s, rows(f), :], TN)
        return jnp.concatenate([face, trace[:, :LANES], trace[:, LANES:], index], axis=0)

    put_faces(faces, canon)

    def density(g, j):
        within = (g >= 0) & (g < n_grp) & (j >= 0) & (j < chain)
        at = jnp.where(within, g * chain + j, 0)
        return jnp.where(within, counts[at].astype(F32) + 1.0, 0.0)

    counts.wait([0])
    for s in range(2):
        j = 2 * sub + s
        own = jnp.full((1, LANES), density(grp, j), F32)
        near = ((grp - 1, j), (grp + 1, j), (grp, j - 1), (grp, j + 1))
        for f, (g, k) in enumerate(near):
            beside = jnp.full((1, LANES), density(g, k), F32)
            weights[pl.ds(4 * s + f, 1), :] = own / (own + beside)
            weights[pl.ds(ACROSS + 4 * s + f, 1), :] = beside / (own + beside)
    base[...] = loads[...]
    for s in range(2):
        padded = [own_basis[s].astype(F32), jnp.zeros((SLOT - SUMS, 4 * FACE), F32)]
        basis[s] = jnp.concatenate(padded, axis=0).astype(BF16)


def settle_kernel(own, other, neumann, high, low, kept, done):
    copy = pltpu.make_async_copy(neumann, kept, done.at[0])
    copy.start()
    upper = odd_core() == 1
    for half in range(2):
        at = pl.ds(half * LANES, LANES)
        mine, theirs = own[...], other[...]
        value = jnp.where(upper, mine, theirs) if half else jnp.where(upper, theirs, mine)
        first, second = split(value)
        high[at, :] = first
        low[at, :] = second
    copy.wait()


def put_message(message, values, start):
    flat = jnp.transpose(values)
    owners = LANES // COLS
    for c in range(COLS):
        message[pl.ds(start + c, owners, stride=TILE), :] = flat[c * owners : (c + 1) * owners]


def get_message(message, start):
    owners = LANES // COLS
    flat = jnp.concatenate(
        [message[pl.ds(start + c, owners, stride=TILE), :] for c in range(COLS)], axis=0
    )
    return jnp.transpose(flat)


def residual_kernel(
    order, inside, other_core, other_slab, core, slab, weights, base, basis, neumann,
    local, traces, message, *faces,
):
    recv = (slab, other_slab, core, other_core, inside)
    moments = []
    scaled = []
    for s in range(2):
        pieces = []
        for f in range(4):
            at = order[4 * s + f]
            beside = dot(at, partner(recv, s, f, WHOLE).astype(BF16))
            value = base[s, rows(f), :].astype(F32) + beside
            pieces.append((share_of(weights, s, f) * value).astype(BF16))
            left = partner(recv, s, f, pl.ds(FACE, 24))
            right = partner(recv, s, f, pl.ds(FACE + 24, 24))
            trace = dot(jnp.concatenate([left, right], axis=1).astype(BF16), at, NT)
            both = [
                basis[s, :, rows(f)].astype(F32), trace, jnp.zeros((SLOT - SUMS, FACE), F32)
            ]
            traces[4 * s + f] = jnp.concatenate(both, axis=0).astype(BF16)
        scaled.append(jnp.concatenate(pieces, axis=0))
        moments.append(dot(basis[s], scaled[s]))
    moments.append(jnp.zeros((LANES - 2 * SLOT, LANES), F32))
    put_message(message, jnp.concatenate(moments, axis=0), 0)
    tile = pl.ds(FACE + 48, TILE)
    own = inside[0, tile, :][0:1]
    lower = partner(recv, 0, 0, tile)[0:1]
    upper = partner(recv, 0, 1, tile)[0:1]
    previous = partner(recv, 0, 2, tile)[0:1]
    following = partner(recv, 1, 3, tile)[0:1]
    first = jnp.concatenate([own[:, : 2 * SLOT], lower[:, : 2 * SLOT]], axis=1)
    second = jnp.concatenate(
        [upper[:, : 2 * SLOT], previous[:, SLOT : 2 * SLOT], following[:, :SLOT]], axis=1
    )
    owners = LANES // COLS
    for c, line in ((COLS, first), (COLS + 1, second)):
        message[pl.ds(c, owners, stride=TILE), :] = jnp.broadcast_to(line, (owners, LANES))
    for c in range(COLS + 2, TILE):
        message[pl.ds(c, owners, stride=TILE), :] = jnp.zeros((owners, LANES), F32)
    send(traces)

    def canon(s, f):
        return to_canon(order[4 * s + f], local[s, rows(f), :])

    for s in range(2):
        product = dot(neumann[s], scaled[s])
        for f in range(4):
            part = product[f * FACE : f * FACE + FACE]
            local[s, rows(f), :] = share_of(weights, s, f) * part
        send(local, s)
        put_slab_faces(faces, canon, s)
    put_core_faces(faces, canon)


def high_low(maps, row):
    at = maps[pl.ds(row, 1), :].astype(jnp.int32)
    return at >> 7, at & (LANES - 1)


def scatter(received, maps, row_at, gathered, lhs, hot, lines):
    owners = received.shape[0] // TILE
    row = lax.broadcasted_iota(jnp.int32, (LANES, LANES), 0)
    tile_row = lax.broadcasted_iota(jnp.int32, (TILE, LANES), 0)
    total = jnp.zeros((TILE, LANES), F32)
    for d in range(owners):
        block = received[pl.ds(TILE * d, TILE), :]
        total = total + block
        span = pl.ds(d * LANES, LANES)
        highs = []
        for line in range(lines):
            high, low = high_low(maps, row_at(d, line))
            highs.append(high)
            hot[pl.ds(line * LANES, LANES), span] = (row == low).astype(F32).astype(BF16)
        high = highs[0]
        if lines == 2:
            high = jnp.where(tile_row < COLS, highs[0], highs[1])
        spread = jnp.concatenate([jnp.where(high == h, block, 0.0) for h in range(HI)], axis=0)
        first, second = split(spread)
        lhs[pl.ds(0, LANES), span] = first
        lhs[pl.ds(LANES, LANES), span] = second
    both = dot(lhs[...], hot[pl.ds(0, lines * LANES), :], NT)
    both = both[:LANES] + both[LANES:]
    packed = []
    for h in range(HI):
        value = both[TILE * h : TILE * h + COLS, :LANES]
        if lines == 2:
            value = value + both[TILE * h + COLS : TILE * h + TILE, LANES:]
        packed.append(value)
    packed = jnp.concatenate(packed + [total], axis=0)
    for z in range(gathered.shape[0] // GATHER):
        gathered[pl.ds(GATHER * z, GATHER), :] = packed


def scatter_kernel(received, gathered, maps, lhs, hot):
    for d in range(received.shape[0] // TILE):
        maps[pl.ds(2 * d, 2), :] = received[pl.ds(TILE * d + COLS, 2), :]
    send(maps)
    scatter(received, received, lambda d, k: TILE * d + COLS + k, gathered, lhs, hot, 1)


def coarse_kernel(gathered, high, low, slab, scalars):
    n_z = gathered.shape[0] // GATHER
    total = gathered[pl.ds(0, GATHER), :]
    for z in range(1, n_z):
        total = total + gathered[pl.ds(GATHER * z, GATHER), :]
    scalars[...] = total[HI * COLS :]
    flat = jnp.concatenate([total[COLS * h : COLS * h + COLS] for h in range(HI)], axis=1)
    first, second = split(flat)
    both = dot(jnp.concatenate([first, second], axis=0), high[...], NT)
    result = both[:COLS] + both[COLS:] + dot(first, low[...], NT)
    tile = jnp.concatenate([result[:, :LANES], result[:, LANES:]], axis=0)
    for z in range(n_z):
        slab[pl.ds(TILE * z, TILE), :] = tile


def pick_kernel(coarse, maps, scalars, message):
    owners = maps.shape[0] // 2
    row = lax.broadcasted_iota(jnp.int32, (LANES, LANES), 0)
    tile_row = lax.broadcasted_iota(jnp.int32, (TILE, LANES), 0)
    lane = lax.broadcasted_iota(jnp.int32, (TILE, LANES), 1)
    carried = (lane >= SUMS) & (lane < SLOT) & (tile_row < COLS)
    first, second = split(coarse[...])
    table = jnp.concatenate([first, second], axis=0)
    extra = scalars[...]
    for d in range(owners):
        pair = [high_low(maps, 2 * d + line) for line in range(2)]
        hot = jnp.concatenate(
            [(row == low).astype(F32).astype(BF16) for _, low in pair], axis=1
        )
        both = dot(table, hot)
        both = both[: HI * COLS] + both[HI * COLS :]
        picked = []
        for line, (high, _) in enumerate(pair):
            value = both[:, line * LANES : line * LANES + LANES]
            total = jnp.zeros((TILE, LANES), F32)
            for v in range(HI * COLS // TILE):
                here = high == (tile_row // COLS + 2 * v)
                total = total + jnp.where(here, value[TILE * v : TILE * v + TILE], 0.0)
            picked.append(total + pltpu.roll(total, COLS, 0))
        value = jnp.where(tile_row < COLS, picked[0], picked[1])
        message[pl.ds(TILE * d, TILE), :] = jnp.where(carried, extra, value)


def slots(message):
    first, second = get_message(message, 0), get_message(message, COLS)
    return [v[SLOT * i : SLOT * i + SLOT] for v in (first, second) for i in range(4)]


def neighbour(s, f):
    if f < 2:
        return 2 + 2 * f + s
    if s == f - 2:
        return 6 + s
    return 1 - s


def spread(traces, weights, picked, s, f):
    both = jnp.concatenate(
        [share_of(weights, s, f) * picked[s], across_of(weights, s, f) * picked[neighbour(s, f)]], axis=0
    )
    return fold(dot(traces[4 * s + f], wide(both), TN))


def column_sum(value):
    return jnp.sum(value, axis=0, keepdims=True)


def direction_kernel(
    returned, dof, traces, weights, local, inside, other_core, other_slab, core, slab, loads,
    schur,
    direction, image, message, *rest,
):
    faces, order = rest[:5], rest[5]
    put_order(order, dof)
    recv = (slab, other_slab, core, other_core, inside)
    picked = slots(returned)
    sums = [jnp.zeros((SLOT, LANES), F32) for _ in range(8)]
    rz = jnp.zeros((1, LANES), F32)
    curve = jnp.zeros((1, LANES), F32)

    def canon(s, f):
        return to_canon(order[4 * s + f], image[s, rows(f), :])

    for s in range(2):
        for f in range(4):
            value = local[s, rows(f), :] + spread(traces, weights, picked, s, f)
            value = value + to_local(order[4 * s + f], partner(recv, s, f, WHOLE))
            direction[s, rows(f), :] = value
            rz = rz + column_sum(loads[s, rows(f), :].astype(F32) * value)
        whole = direction[s]
        product = dot(schur[s], whole.astype(BF16))
        image[s] = product
        curve = curve + column_sum(whole * product)
        send(direction, s)
        send(image, s)
        put_slab_faces(faces, canon, s)
    put_core_faces(faces, canon)
    for s in range(2):
        for f in range(4):
            both = fold(dot(traces[4 * s + f], wide(image[s, rows(f), :])))
            sums[s] = sums[s] + share_of(weights, s, f) * both[:SLOT]
            to = neighbour(s, f)
            sums[to] = sums[to] + across_of(weights, s, f) * both[SLOT:]
    carried = [rz, curve, jnp.zeros((SLOT - SUMS - 2, LANES), F32)]
    first = [sums[0][:SUMS]] + carried + sums[1:4]
    put_message(message, jnp.concatenate(first, axis=0), 0)
    put_message(message, jnp.concatenate(sums[4:], axis=0), COLS)


def image_kernel(
    received, maps, dof, weights, partial, inside, other_core, other_slab, core, slab, neumann,
    gathered, local, *rest,
):
    faces, (lhs, hot, order) = rest[:5], rest[5:]
    put_order(order, dof)
    recv = (slab, other_slab, core, other_core, inside)
    scatter(received, maps, lambda d, k: 2 * d + k, gathered, lhs, hot, 2)

    def canon(s, f):
        return to_canon(order[4 * s + f], local[s, rows(f), :])

    for s in range(2):
        pieces = []
        for f in range(4):
            beside = to_local(order[4 * s + f], partner(recv, s, f, WHOLE))
            value = partial[s, rows(f), :] + beside
            pieces.append(wide(share_of(weights, s, f) * value))
        product = fold(dot(neumann[s], jnp.concatenate(pieces, axis=0)))
        for f in range(4):
            part = product[f * FACE : f * FACE + FACE]
            local[s, rows(f), :] = share_of(weights, s, f) * part
        send(local, s)
        put_slab_faces(faces, canon, s)
    put_core_faces(faces, canon)


def last_kernel(
    returned, dof, traces, weights, local, inside, other_core, other_slab, core, slab, direction,
    loads, schur,
    search, scalars, message, order,
):
    put_order(order, dof)
    recv = (slab, other_slab, core, other_core, inside)
    picked = slots(returned)
    carried = picked[0][SUMS : SUMS + 2]
    rz, curve = carried[0:1], carried[1:2]
    step = rz / curve
    scalars[...] = jnp.concatenate([rz, curve, step, jnp.zeros((TILE - 3, LANES), F32)], axis=0)
    along = jnp.zeros((1, LANES), F32)
    same = jnp.zeros((1, LANES), F32)
    cross = jnp.zeros((1, LANES), F32)
    for s in range(2):
        for f in range(4):
            value = local[s, rows(f), :] + spread(traces, weights, picked, s, f)
            value = value + to_local(order[4 * s + f], partner(recv, s, f, WHOLE))
            value = direction[s, rows(f), :] - step * value
            search[s, rows(f), :] = value
            along = along + column_sum(loads[s, rows(f), :].astype(F32) * value)
        whole = search[s]
        send(search, s)
        rounded = whole.astype(BF16)
        product = dot(schur[s], rounded)
        twice = 2.0 * whole - rounded.astype(F32)
        same = same + column_sum(twice * product)
        cross = cross + column_sum(direction[s] * product)
    rz_next = along - step * cross
    tile = jnp.concatenate([rz_next, same, cross, jnp.zeros((TILE - 3, LANES), F32)], axis=0)
    for d in range(message.shape[0] // TILE):
        message[pl.ds(TILE * d, TILE), :] = tile


def sum_tiles(received):
    total = received[pl.ds(0, TILE), :]
    for d in range(1, received.shape[0] // TILE):
        total = total + received[pl.ds(TILE * d, TILE), :]
    return total


def sum_kernel(received, out):
    total = sum_tiles(received)
    for z in range(out.shape[0] // TILE):
        out[pl.ds(TILE * z, TILE), :] = total


def finish_kernel(received, scalars, direction, search, out):
    total = sum_tiles(received)
    rz, curve, step = scalars[0:1, :], scalars[1:2, :], scalars[2:3, :]
    rz_next, same, cross = total[0:1], total[1:2], total[2:3]
    beta = rz_next / rz
    curve_next = same + 2.0 * beta * cross + beta * beta * curve
    step_next = rz_next / curve_next
    along = step + step_next * beta
    for s in range(2):
        out[s] = along * direction[s] + step_next * search[s]
        send(out, s)


def settle(own, other, neumann):
    return pl.pallas_call(
        settle_body,
        out_shape=[
            jax.ShapeDtypeStruct((2 * LANES, own.shape[1]), BF16),
            jax.ShapeDtypeStruct((2 * LANES, own.shape[1]), BF16),
            jax.ShapeDtypeStruct(neumann.shape, BF16),
        ],
        in_specs=[pl.BlockSpec(memory_space=pl.ANY)] * 3,
        out_specs=[pl.BlockSpec(memory_space=pltpu.VMEM)] * 3,
        scratch_shapes=[
            pltpu.VMEM(own.shape, F32),
            pltpu.VMEM(own.shape, F32),
            pltpu.SemaphoreType.DMA((1,)),
            pltpu.SemaphoreType.DMA((1,)),
            pltpu.SemaphoreType.DMA((1,)),
        ],
        compiler_params=pltpu.CompilerParams(vmem_limit_bytes=VMEM_LIMIT),
    )(
        pltpu.with_memory_space_constraint(own, pltpu.HBM),
        other,
        pltpu.with_memory_space_constraint(neumann, pltpu.HBM),
    )


def settle_body(own, other, neumann, high, low, kept, own_here, other_here, a, b, c):
    fetched = Fetched(own, own_here, a), Fetched(other, other_here, b)
    settle_kernel(*fetched, neumann, high, low, kept, c)


def body(loads, schur, neumann, basis, dof_order, primal_map, emitter_counts, coarse_inverse):
    n_grp = lax.axis_size("grp")
    n_sub = lax.axis_size("sub")
    n_z = n_sub // 2
    vector = Far((2, 4 * FACE, LANES))
    small = Near((TILE, LANES))
    owners = 2 * n_grp
    message_shape = Near((owners * TILE, LANES))

    plane = [
        [g * n_sub + 2 * z + c for g in range(n_grp) for c in range(2)] for z in range(n_z)
    ]
    column = [
        [g * n_sub + 2 * z + c for z in range(n_z)] for g in range(n_grp) for c in range(2)
    ]

    def to_owners(value):
        return lax.all_to_all(value, AXES, 0, 0, axis_index_groups=plane, tiled=True)

    def along_z(value):
        return lax.all_to_all(value, AXES, 0, 0, axis_index_groups=column, tiled=True)

    swap = [(i, i ^ 1) for i in range(n_sub)]
    other = lax.ppermute(coarse_inverse, "sub", swap)
    order, weights, base, padded, *faces = call(
        prepare_kernel,
        [
            Near((8, FACE, FACE), BF16),
            Near((2 * TILE, LANES)),
            Near(loads.shape, BF16),
            Near((2, SLOT, 4 * FACE), BF16),
        ]
        + halo_shapes(LONG, Near),
        dof_order, loads, basis, primal_map, emitter_counts,
        far=(0, 1, 2, 3, 4), smem=(4,),
    )

    def halo(faces):
        slab, other_slab, core, other_core, inside = exchange(faces)
        return inside, other_core, other_slab, core, slab

    recv = halo(faces)
    high, low, kept = settle(coarse_inverse, other, neumann)
    one_hot = pltpu.VMEM((8, FACE, FACE), BF16)
    lists = (
        pltpu.VMEM((2 * LANES, owners * LANES), BF16),
        pltpu.VMEM((2 * LANES, owners * LANES), BF16),
    )
    gathered_shape = Near((n_z * GATHER, LANES))

    def coarse_solve(gathered, maps):
        slab, sums = call(
            coarse_kernel, [Near((n_z * TILE, LANES)), small], along_z(gathered), high, low
        )
        (picked,) = call(
            pick_kernel, [message_shape], along_z(slab), maps, sums
        )
        return to_owners(picked)

    local, traces, message, *faces = call(
        residual_kernel,
        [vector, Near((8, 2 * SLOT, FACE), BF16), message_shape] + halo_shapes(FACE, Far),
        order, *recv, weights, base, padded, kept,
    )
    recv = halo(faces)
    gathered, maps = call(
        scatter_kernel, [gathered_shape, Near((2 * owners, LANES))], to_owners(message),
        scratch=lists,
    )
    returned = coarse_solve(gathered, maps)
    direction, partial, message, *faces = call(
        direction_kernel,
        [vector, vector, message_shape] + halo_shapes(FACE, Far),
        returned, dof_order, traces, weights, local, *recv, loads, schur,
        far=[1, 4, 5, 10, 11], scratch=(one_hot,),
    )
    recv = halo(faces)
    gathered, local, *faces = call(
        image_kernel,
        [gathered_shape, vector] + halo_shapes(FACE, Far),
        to_owners(message), maps, dof_order, weights, partial, *recv, neumann,
        far=[2, 4, 5, 10], scratch=lists + (one_hot,),
    )
    recv = halo(faces)
    returned = coarse_solve(gathered, maps)
    search, scalars, message = call(
        last_kernel,
        [vector, small, message_shape],
        returned, dof_order, traces, weights, local, *recv, direction, loads, schur,
        far=[1, 4, 5, 10, 11, 12], scratch=(one_hot,),
    )
    (sums,) = call(sum_kernel, [Near((n_z * TILE, LANES))], to_owners(message))
    (out,) = call(
        finish_kernel, [vector], along_z(sums), scalars, direction, search, far=(2, 3)
    )
    return out


def solution(mesh):
    in_specs = (
        P(AXES, None, None),
        P(AXES, None, None),
        P(AXES, None, None),
        P(AXES, None, None),
        P(AXES, None, None),
        P(AXES, None),
        P(),
        P("sub", None),
    )
    return jax.shard_map(
        body, mesh=mesh, in_specs=in_specs, out_specs=P(AXES, None, None), check_vma=False
    )
```

```python
import functools

import jax
import jax.numpy as jnp
from jax import lax
from jax.experimental import pallas as pl
from jax.experimental.pallas import tpu as pltpu
from jax.sharding import PartitionSpec as P

F32 = jnp.float32
BF16 = jnp.bfloat16
AXES = ("grp", "sub")
LANES = 128
TILE = 8
FACE = 256
HI = 16
COLS = 4
GATHER = HI * COLS + TILE
SLOT = 32
SUMS = 24
ACROSS = 8
VMEM_LIMIT = 40 * 1024 * 1024

NN = (((1,), (0,)), ((), ()))
NT = (((1,), (1,)), ((), ()))
TN = (((0,), (0,)), ((), ()))


def dot(left, right, dims=NN):
    return lax.dot_general(left, right, dims, preferred_element_type=F32)


def split(value):
    high = value.astype(BF16)
    return high, (value - high.astype(F32)).astype(BF16)


def wide(value):
    return jnp.concatenate(split(value), axis=1)


def fold(value):
    return value[:, :LANES] + value[:, LANES:]


def to_canon(order, value):
    return fold(dot(order, wide(value), TN))


def to_local(order, value):
    return fold(dot(order, wide(value)))


def rows(face):
    return pl.ds(pl.multiple_of(face * FACE, FACE), FACE)


class Near:
    def __init__(self, shape, dtype=F32):
        self.shape, self.dtype = tuple(shape), dtype


class Far(Near):
    pass


class Fetched:
    def __init__(self, source, scratch, done):
        self.scratch = scratch
        parts = done.shape[0]
        if parts == 1:
            self.copies = [pltpu.make_async_copy(source, scratch, done.at[0])]
        else:
            self.copies = [
                pltpu.make_async_copy(source.at[i], scratch.at[i], done.at[i])
                for i in range(parts)
            ]
        self.waiting = set(range(parts))
        self.shape = source.shape
        for copy in self.copies:
            copy.start()

    def wait(self, parts):
        for i in sorted(self.waiting & set(parts)):
            self.copies[i].wait()
        self.waiting -= set(parts)

    def __getitem__(self, at):
        first = at[0] if isinstance(at, tuple) else at
        every = range(len(self.copies))
        one = isinstance(first, int) and len(self.copies) > 1
        self.wait([first] if one else every)
        return self.scratch[at]


def send(result, part=None):
    if isinstance(result, Stored):
        result.send(part)


class Stored:
    def __init__(self, target, scratch, done):
        self.scratch, self.shape = scratch, scratch.shape
        parts = done.shape[0]
        if parts == 1:
            self.copies = [pltpu.make_async_copy(scratch, target, done.at[0])]
        else:
            self.copies = [
                pltpu.make_async_copy(scratch.at[i], target.at[i], done.at[i])
                for i in range(parts)
            ]
        self.left = list(range(parts))

    def __setitem__(self, at, value):
        self.scratch[at] = value

    def __getitem__(self, at):
        return self.scratch[at]

    def send(self, part=None):
        for i in list(self.left) if part is None else [part]:
            self.copies[i].start()
            self.left.remove(i)

    def wait(self):
        for copy in self.copies:
            copy.wait()


def parts_of(array):
    return 2 if len(array.shape) == 3 and array.shape[0] == 2 else 1


def call(kernel, outs, *args, far=(), smem=(), loose=(), scratch=()):
    n_in, n_out = len(args), len(outs)
    far_in = list(far)
    far_out = [i for i, out in enumerate(outs) if isinstance(out, Far)]
    extra = []
    for i in far_in:
        kind = pltpu.SMEM if i in smem else pltpu.VMEM
        extra.append(kind(args[i].shape, args[i].dtype))
        extra.append(pltpu.SemaphoreType.DMA((parts_of(args[i]),)))
    for i in far_out:
        extra.append(pltpu.VMEM(outs[i].shape, outs[i].dtype))
        extra.append(pltpu.SemaphoreType.DMA((parts_of(outs[i]),)))

    def whole(*refs):
        ins, results = list(refs[:n_in]), list(refs[n_in : n_in + n_out])
        rest = refs[n_in + n_out :]
        own, rest = rest[: len(scratch)], rest[len(scratch) :]
        for k, i in enumerate(far_in):
            ins[i] = Fetched(ins[i], rest[2 * k], rest[2 * k + 1])
        rest = rest[2 * len(far_in) :]
        for k, i in enumerate(far_out):
            results[i] = Stored(results[i], rest[2 * k], rest[2 * k + 1])
        kernel(*ins, *results, *own)
        for i in far_in:
            ins[i].wait(range(len(ins[i].copies)))
        for i in far_out:
            results[i].send()
        for i in far_out:
            results[i].wait()

    operands = [
        pltpu.with_memory_space_constraint(a, pltpu.HBM) if i in far and i not in loose else a
        for i, a in enumerate(args)
    ]
    return pl.pallas_call(
        whole,
        out_shape=[
            pltpu.HBM(out.shape, out.dtype)
            if isinstance(out, Far)
            else jax.ShapeDtypeStruct(out.shape, out.dtype)
            for out in outs
        ],
        in_specs=[
            pl.BlockSpec(memory_space=pl.ANY if i in far else pltpu.VMEM)
            for i in range(n_in)
        ],
        out_specs=[
            pl.BlockSpec(memory_space=pl.ANY if i in far_out else pltpu.VMEM)
            for i in range(n_out)
        ],
        scratch_shapes=list(scratch) + extra,
        compiler_params=pltpu.CompilerParams(vmem_limit_bytes=VMEM_LIMIT),
    )(*operands)


def odd_slab():
    return lax.axis_index("grp") % 2


def odd_core():
    return lax.axis_index("sub") % 2


def halo_shapes(length, place):
    return [
        place((2, length, LANES)),
        place((2, length, LANES)),
        place((length, LANES)),
        place((length, LANES)),
        place((2, length, LANES)),
    ]


def put_order(order, dof):
    row = lax.broadcasted_iota(jnp.int32, (FACE, FACE), 0)
    for s in range(2):
        for f in range(4):
            order[4 * s + f] = (row == dof[s, pl.ds(f, 1), :]).astype(F32).astype(BF16)


def put_slab_faces(faces, canon, s):
    slab, other_slab = faces[:2]
    odd = odd_slab()
    other_slab[s] = canon(s, odd)
    send(other_slab, s)
    slab[s] = canon(s, 1 - odd)
    send(slab, s)


def put_core_faces(faces, canon):
    core, other_core, inside = faces[2:]
    odd = odd_core()
    other_core[...] = canon(odd, 2 + odd)
    send(other_core)
    core[...] = canon(1 - odd, 3 - odd)
    send(core)
    inside[0] = canon(0, 3)
    inside[1] = canon(1, 2)
    send(inside)


def put_faces(faces, canon):
    for s in range(2):
        put_slab_faces(faces, canon, s)
    put_core_faces(faces, canon)


def partner(recv, s, f, span):
    slab, other_slab, core, other_core, inside = recv
    if f < 2:
        here, there = slab[s, span, :], other_slab[s, span, :]
        return jnp.where(odd_slab() == f, there, here)
    if s != f - 2:
        return inside[1 - s, span, :]
    here, there = core[span, :], other_core[span, :]
    return jnp.where(odd_core() == 1 - s, here, there)


WHOLE = pl.ds(0, FACE)


def exchange(send):
    slab, other_slab, core, other_core, inside = send
    n_grp = lax.axis_size("grp")
    n_sub = lax.axis_size("sub")

    def pairs(count, first):
        steps = [(i, i + 1) for i in range(first, count - 1, 2)]
        return steps + [(j, i) for i, j in steps]

    other_core = lax.ppermute(other_core, "sub", pairs(n_sub, 1))
    other_slab = lax.ppermute(other_slab, "grp", pairs(n_grp, 1))
    slab = lax.ppermute(slab, "grp", pairs(n_grp, 0))
    core = lax.ppermute(core, "sub", pairs(n_sub, 0))
    return [slab, other_slab, core, other_core, inside]


def share_of(weights, s, f):
    return weights[pl.ds(4 * s + f, 1), :]


def across_of(weights, s, f):
    return weights[pl.ds(ACROSS + 4 * s + f, 1), :]


LONG = FACE + 2 * 24 + TILE


def prepare_kernel(
    dof, loads, own_basis, primal, counts,
    order, weights, base, basis, *faces,
):
    grp, sub = lax.axis_index("grp"), lax.axis_index("sub")
    n_grp, n_sub = lax.axis_size("grp"), lax.axis_size("sub")
    chain = 2 * n_sub
    put_order(order, dof)
    index = primal[...].astype(F32)
    pad = jnp.full((1, SLOT - SUMS), -1.0, F32)
    index = jnp.concatenate(
        [index[0:1], pad, index[1:2], pad, jnp.zeros((1, LANES - 2 * SLOT), F32)], axis=1
    )
    index = jnp.broadcast_to(index, (TILE, LANES))
    loads.wait(range(2))
    own_basis.wait(range(2))

    def canon(s, f):
        at = order[4 * s + f]
        trace = dot(own_basis.scratch[s, :, rows(f)], at)
        face = dot(at, loads.scratch[s, rows(f), :], TN)
        return jnp.concatenate([face, trace[:, :LANES], trace[:, LANES:], index], axis=0)

    put_faces(faces, canon)

    def density(g, j):
        within = (g >= 0) & (g < n_grp) & (j >= 0) & (j < chain)
        at = jnp.where(within, g * chain + j, 0)
        return jnp.where(within, counts[at].astype(F32) + 1.0, 0.0)

    counts.wait([0])
    for s in range(2):
        j = 2 * sub + s
        own = jnp.full((1, LANES), density(grp, j), F32)
        near = ((grp - 1, j), (grp + 1, j), (grp, j - 1), (grp, j + 1))
        for f, (g, k) in enumerate(near):
            beside = jnp.full((1, LANES), density(g, k), F32)
            weights[pl.ds(4 * s + f, 1), :] = own / (own + beside)
            weights[pl.ds(ACROSS + 4 * s + f, 1), :] = beside / (own + beside)
    base[...] = loads[...]
    for s in range(2):
        padded = [own_basis[s].astype(F32), jnp.zeros((SLOT - SUMS, 4 * FACE), F32)]
        basis[s] = jnp.concatenate(padded, axis=0).astype(BF16)


def settle_kernel(own, other, neumann, high, low, kept, done):
    copy = pltpu.make_async_copy(neumann, kept, done.at[0])
    copy.start()
    upper = odd_core() == 1
    for half in range(2):
        at = pl.ds(half * LANES, LANES)
        mine, theirs = own[...], other[...]
        value = jnp.where(upper, mine, theirs) if half else jnp.where(upper, theirs, mine)
        first, second = split(value)
        high[at, :] = first
        low[at, :] = second
    copy.wait()


def put_message(message, values, start):
    flat = jnp.transpose(values)
    owners = LANES // COLS
    for c in range(COLS):
        message[pl.ds(start + c, owners, stride=TILE), :] = flat[c * owners : (c + 1) * owners]


def get_message(message, start):
    owners = LANES // COLS
    flat = jnp.concatenate(
        [message[pl.ds(start + c, owners, stride=TILE), :] for c in range(COLS)], axis=0
    )
    return jnp.transpose(flat)


def residual_kernel(
    order, inside, other_core, other_slab, core, slab, weights, base, basis, neumann,
    local, traces, message, *faces,
):
    recv = (slab, other_slab, core, other_core, inside)
    moments = []
    scaled = []
    for s in range(2):
        pieces = []
        for f in range(4):
            at = order[4 * s + f]
            beside = dot(at, partner(recv, s, f, WHOLE).astype(BF16))
            value = base[s, rows(f), :].astype(F32) + beside
            pieces.append((share_of(weights, s, f) * value).astype(BF16))
            left = partner(recv, s, f, pl.ds(FACE, 24))
            right = partner(recv, s, f, pl.ds(FACE + 24, 24))
            trace = dot(jnp.concatenate([left, right], axis=1).astype(BF16), at, NT)
            both = [
                basis[s, :, rows(f)].astype(F32), trace, jnp.zeros((SLOT - SUMS, FACE), F32)
            ]
            traces[4 * s + f] = jnp.concatenate(both, axis=0).astype(BF16)
        scaled.append(jnp.concatenate(pieces, axis=0))
        moments.append(dot(basis[s], scaled[s]))
    moments.append(jnp.zeros((LANES - 2 * SLOT, LANES), F32))
    put_message(message, jnp.concatenate(moments, axis=0), 0)
    tile = pl.ds(FACE + 48, TILE)
    own = inside[0, tile, :][0:1]
    lower = partner(recv, 0, 0, tile)[0:1]
    upper = partner(recv, 0, 1, tile)[0:1]
    previous = partner(recv, 0, 2, tile)[0:1]
    following = partner(recv, 1, 3, tile)[0:1]
    first = jnp.concatenate([own[:, : 2 * SLOT], lower[:, : 2 * SLOT]], axis=1)
    second = jnp.concatenate(
        [upper[:, : 2 * SLOT], previous[:, SLOT : 2 * SLOT], following[:, :SLOT]], axis=1
    )
    owners = LANES // COLS
    for c, line in ((COLS, first), (COLS + 1, second)):
        message[pl.ds(c, owners, stride=TILE), :] = jnp.broadcast_to(line, (owners, LANES))
    for c in range(COLS + 2, TILE):
        message[pl.ds(c, owners, stride=TILE), :] = jnp.zeros((owners, LANES), F32)
    send(traces)

    def canon(s, f):
        return to_canon(order[4 * s + f], local[s, rows(f), :])

    for s in range(2):
        product = dot(neumann[s], scaled[s])
        for f in range(4):
            part = product[f * FACE : f * FACE + FACE]
            local[s, rows(f), :] = share_of(weights, s, f) * part
        send(local, s)
        put_slab_faces(faces, canon, s)
    put_core_faces(faces, canon)


def high_low(maps, row):
    at = maps[pl.ds(row, 1), :].astype(jnp.int32)
    return at >> 7, at & (LANES - 1)


def scatter(received, maps, row_at, gathered, lhs, hot, lines):
    owners = received.shape[0] // TILE
    row = lax.broadcasted_iota(jnp.int32, (LANES, LANES), 0)
    tile_row = lax.broadcasted_iota(jnp.int32, (TILE, LANES), 0)
    total = jnp.zeros((TILE, LANES), F32)
    for d in range(owners):
        block = received[pl.ds(TILE * d, TILE), :]
        total = total + block
        span = pl.ds(d * LANES, LANES)
        highs = []
        for line in range(lines):
            high, low = high_low(maps, row_at(d, line))
            highs.append(high)
            hot[pl.ds(line * LANES, LANES), span] = (row == low).astype(F32).astype(BF16)
        high = highs[0]
        if lines == 2:
            high = jnp.where(tile_row < COLS, highs[0], highs[1])
        spread = jnp.concatenate([jnp.where(high == h, block, 0.0) for h in range(HI)], axis=0)
        first, second = split(spread)
        lhs[pl.ds(0, LANES), span] = first
        lhs[pl.ds(LANES, LANES), span] = second
    both = dot(lhs[...], hot[pl.ds(0, lines * LANES), :], NT)
    both = both[:LANES] + both[LANES:]
    packed = []
    for h in range(HI):
        value = both[TILE * h : TILE * h + COLS, :LANES]
        if lines == 2:
            value = value + both[TILE * h + COLS : TILE * h + TILE, LANES:]
        packed.append(value)
    packed = jnp.concatenate(packed + [total], axis=0)
    for z in range(gathered.shape[0] // GATHER):
        gathered[pl.ds(GATHER * z, GATHER), :] = packed


def scatter_kernel(received, gathered, maps, lhs, hot):
    for d in range(received.shape[0] // TILE):
        maps[pl.ds(2 * d, 2), :] = received[pl.ds(TILE * d + COLS, 2), :]
    send(maps)
    scatter(received, received, lambda d, k: TILE * d + COLS + k, gathered, lhs, hot, 1)


def scatter_both_kernel(received, maps, gathered, lhs, hot):
    scatter(received, maps, lambda d, k: 2 * d + k, gathered, lhs, hot, 2)


def coarse_kernel(gathered, high, low, slab, scalars):
    n_z = gathered.shape[0] // GATHER
    total = gathered[pl.ds(0, GATHER), :]
    for z in range(1, n_z):
        total = total + gathered[pl.ds(GATHER * z, GATHER), :]
    scalars[...] = total[HI * COLS :]
    flat = jnp.concatenate([total[COLS * h : COLS * h + COLS] for h in range(HI)], axis=1)
    first, second = split(flat)
    both = dot(jnp.concatenate([first, second], axis=0), high[...], NT)
    result = both[:COLS] + both[COLS:] + dot(first, low[...], NT)
    tile = jnp.concatenate([result[:, :LANES], result[:, LANES:]], axis=0)
    for z in range(n_z):
        slab[pl.ds(TILE * z, TILE), :] = tile


def pick_kernel(coarse, maps, scalars, message):
    owners = maps.shape[0] // 2
    row = lax.broadcasted_iota(jnp.int32, (LANES, LANES), 0)
    tile_row = lax.broadcasted_iota(jnp.int32, (TILE, LANES), 0)
    lane = lax.broadcasted_iota(jnp.int32, (TILE, LANES), 1)
    carried = (lane >= SUMS) & (lane < SLOT) & (tile_row < COLS)
    first, second = split(coarse[...])
    table = jnp.concatenate([first, second], axis=0)
    extra = scalars[...]
    for d in range(owners):
        pair = [high_low(maps, 2 * d + line) for line in range(2)]
        hot = jnp.concatenate(
            [(row == low).astype(F32).astype(BF16) for _, low in pair], axis=1
        )
        both = dot(table, hot)
        both = both[: HI * COLS] + both[HI * COLS :]
        picked = []
        for line, (high, _) in enumerate(pair):
            value = both[:, line * LANES : line * LANES + LANES]
            total = jnp.zeros((TILE, LANES), F32)
            for v in range(HI * COLS // TILE):
                here = high == (tile_row // COLS + 2 * v)
                total = total + jnp.where(here, value[TILE * v : TILE * v + TILE], 0.0)
            picked.append(total + pltpu.roll(total, COLS, 0))
        value = jnp.where(tile_row < COLS, picked[0], picked[1])
        message[pl.ds(TILE * d, TILE), :] = jnp.where(carried, extra, value)


def slots(message):
    first, second = get_message(message, 0), get_message(message, COLS)
    return [v[SLOT * i : SLOT * i + SLOT] for v in (first, second) for i in range(4)]


def neighbour(s, f):
    if f < 2:
        return 2 + 2 * f + s
    if s == f - 2:
        return 6 + s
    return 1 - s


def spread(traces, weights, picked, s, f):
    both = jnp.concatenate(
        [share_of(weights, s, f) * picked[s], across_of(weights, s, f) * picked[neighbour(s, f)]], axis=0
    )
    return fold(dot(traces[4 * s + f], wide(both), TN))


def column_sum(value):
    return jnp.sum(value, axis=0, keepdims=True)


def direction_kernel(
    returned, dof, traces, weights, local, inside, other_core, other_slab, core, slab, loads,
    schur,
    direction, image, message, *rest,
):
    faces, order = rest[:5], rest[5]
    put_order(order, dof)
    recv = (slab, other_slab, core, other_core, inside)
    picked = slots(returned)
    sums = [jnp.zeros((SLOT, LANES), F32) for _ in range(8)]
    rz = jnp.zeros((1, LANES), F32)
    curve = jnp.zeros((1, LANES), F32)

    def canon(s, f):
        return to_canon(order[4 * s + f], image[s, rows(f), :])

    for s in range(2):
        for f in range(4):
            value = local[s, rows(f), :] + spread(traces, weights, picked, s, f)
            value = value + to_local(order[4 * s + f], partner(recv, s, f, WHOLE))
            direction[s, rows(f), :] = value
            rz = rz + column_sum(loads[s, rows(f), :].astype(F32) * value)
        whole = direction[s]
        product = dot(schur[s], whole.astype(BF16))
        image[s] = product
        curve = curve + column_sum(whole * product)
        send(direction, s)
        send(image, s)
        put_slab_faces(faces, canon, s)
    put_core_faces(faces, canon)
    for s in range(2):
        for f in range(4):
            both = fold(dot(traces[4 * s + f], wide(image[s, rows(f), :])))
            sums[s] = sums[s] + share_of(weights, s, f) * both[:SLOT]
            to = neighbour(s, f)
            sums[to] = sums[to] + across_of(weights, s, f) * both[SLOT:]
    carried = [rz, curve, jnp.zeros((SLOT - SUMS - 2, LANES), F32)]
    first = [sums[0][:SUMS]] + carried + sums[1:4]
    put_message(message, jnp.concatenate(first, axis=0), 0)
    put_message(message, jnp.concatenate(sums[4:], axis=0), COLS)


def image_kernel(
    received, dof, weights, partial, inside, other_core, other_slab, core, slab, neumann,
    local, *rest,
):
    faces, order = rest[:5], rest[5]
    put_order(order, dof)
    recv = (slab, other_slab, core, other_core, inside)

    def canon(s, f):
        return to_canon(order[4 * s + f], local[s, rows(f), :])

    for s in range(2):
        pieces = []
        for f in range(4):
            beside = to_local(order[4 * s + f], partner(recv, s, f, WHOLE))
            value = partial[s, rows(f), :] + beside
            pieces.append(wide(share_of(weights, s, f) * value))
        product = fold(dot(neumann[s], jnp.concatenate(pieces, axis=0)))
        for f in range(4):
            part = product[f * FACE : f * FACE + FACE]
            local[s, rows(f), :] = share_of(weights, s, f) * part
        send(local, s)
        put_slab_faces(faces, canon, s)
    put_core_faces(faces, canon)


def last_kernel(
    returned, dof, traces, weights, local, inside, other_core, other_slab, core, slab, direction,
    loads, schur,
    search, scalars, message, order,
):
    put_order(order, dof)
    recv = (slab, other_slab, core, other_core, inside)
    picked = slots(returned)
    carried = picked[0][SUMS : SUMS + 2]
    rz, curve = carried[0:1], carried[1:2]
    step = rz / curve
    scalars[...] = jnp.concatenate([rz, curve, step, jnp.zeros((TILE - 3, LANES), F32)], axis=0)
    along = jnp.zeros((1, LANES), F32)
    same = jnp.zeros((1, LANES), F32)
    cross = jnp.zeros((1, LANES), F32)
    for s in range(2):
        for f in range(4):
            value = local[s, rows(f), :] + spread(traces, weights, picked, s, f)
            value = value + to_local(order[4 * s + f], partner(recv, s, f, WHOLE))
            value = direction[s, rows(f), :] - step * value
            search[s, rows(f), :] = value
            along = along + column_sum(loads[s, rows(f), :].astype(F32) * value)
        whole = search[s]
        send(search, s)
        rounded = whole.astype(BF16)
        product = dot(schur[s], rounded)
        twice = 2.0 * whole - rounded.astype(F32)
        same = same + column_sum(twice * product)
        cross = cross + column_sum(direction[s] * product)
    rz_next = along - step * cross
    tile = jnp.concatenate([rz_next, same, cross, jnp.zeros((TILE - 3, LANES), F32)], axis=0)
    for d in range(message.shape[0] // TILE):
        message[pl.ds(TILE * d, TILE), :] = tile


def sum_tiles(received):
    total = received[pl.ds(0, TILE), :]
    for d in range(1, received.shape[0] // TILE):
        total = total + received[pl.ds(TILE * d, TILE), :]
    return total


def sum_kernel(received, out):
    total = sum_tiles(received)
    for z in range(out.shape[0] // TILE):
        out[pl.ds(TILE * z, TILE), :] = total


def finish_kernel(received, scalars, direction, search, out):
    total = sum_tiles(received)
    rz, curve, step = scalars[0:1, :], scalars[1:2, :], scalars[2:3, :]
    rz_next, same, cross = total[0:1], total[1:2], total[2:3]
    beta = rz_next / rz
    curve_next = same + 2.0 * beta * cross + beta * beta * curve
    step_next = rz_next / curve_next
    along = step + step_next * beta
    for s in range(2):
        out[s] = along * direction[s] + step_next * search[s]
        send(out, s)


def settle(own, other, neumann):
    return pl.pallas_call(
        settle_body,
        out_shape=[
            jax.ShapeDtypeStruct((2 * LANES, own.shape[1]), BF16),
            jax.ShapeDtypeStruct((2 * LANES, own.shape[1]), BF16),
            jax.ShapeDtypeStruct(neumann.shape, BF16),
        ],
        in_specs=[pl.BlockSpec(memory_space=pl.ANY)] * 3,
        out_specs=[pl.BlockSpec(memory_space=pltpu.VMEM)] * 3,
        scratch_shapes=[
            pltpu.VMEM(own.shape, F32),
            pltpu.VMEM(own.shape, F32),
            pltpu.SemaphoreType.DMA((1,)),
            pltpu.SemaphoreType.DMA((1,)),
            pltpu.SemaphoreType.DMA((1,)),
        ],
        compiler_params=pltpu.CompilerParams(vmem_limit_bytes=VMEM_LIMIT),
    )(
        pltpu.with_memory_space_constraint(own, pltpu.HBM),
        other,
        pltpu.with_memory_space_constraint(neumann, pltpu.HBM),
    )


def settle_body(own, other, neumann, high, low, kept, own_here, other_here, a, b, c):
    fetched = Fetched(own, own_here, a), Fetched(other, other_here, b)
    settle_kernel(*fetched, neumann, high, low, kept, c)


def body(loads, schur, neumann, basis, dof_order, primal_map, emitter_counts, coarse_inverse):
    n_grp = lax.axis_size("grp")
    n_sub = lax.axis_size("sub")
    n_z = n_sub // 2
    vector = Far((2, 4 * FACE, LANES))
    small = Near((TILE, LANES))
    owners = 2 * n_grp
    message_shape = Near((owners * TILE, LANES))

    plane = [
        [g * n_sub + 2 * z + c for g in range(n_grp) for c in range(2)] for z in range(n_z)
    ]
    column = [
        [g * n_sub + 2 * z + c for z in range(n_z)] for g in range(n_grp) for c in range(2)
    ]

    def to_owners(value):
        return lax.all_to_all(value, AXES, 0, 0, axis_index_groups=plane, tiled=True)

    def along_z(value):
        return lax.all_to_all(value, AXES, 0, 0, axis_index_groups=column, tiled=True)

    swap = [(i, i ^ 1) for i in range(n_sub)]
    other = lax.ppermute(coarse_inverse, "sub", swap)
    order, weights, base, padded, *faces = call(
        prepare_kernel,
        [
            Near((8, FACE, FACE), BF16),
            Near((2 * TILE, LANES)),
            Near(loads.shape, BF16),
            Near((2, SLOT, 4 * FACE), BF16),
        ]
        + halo_shapes(LONG, Near),
        dof_order, loads, basis, primal_map, emitter_counts,
        far=(0, 1, 2, 3, 4), smem=(4,),
    )

    def halo(faces):
        slab, other_slab, core, other_core, inside = exchange(faces)
        return inside, other_core, other_slab, core, slab

    recv = halo(faces)
    high, low, kept = settle(coarse_inverse, other, neumann)
    one_hot = pltpu.VMEM((8, FACE, FACE), BF16)
    lists = (
        pltpu.VMEM((2 * LANES, owners * LANES), BF16),
        pltpu.VMEM((2 * LANES, owners * LANES), BF16),
    )
    gathered_shape = Near((n_z * GATHER, LANES))

    def coarse_solve(gathered, maps):
        slab, sums = call(
            coarse_kernel, [Near((n_z * TILE, LANES)), small], along_z(gathered), high, low
        )
        (picked,) = call(
            pick_kernel, [message_shape], along_z(slab), maps, sums
        )
        return to_owners(picked)

    local, traces, message, *faces = call(
        residual_kernel,
        [vector, Near((8, 2 * SLOT, FACE), BF16), message_shape] + halo_shapes(FACE, Far),
        order, *recv, weights, base, padded, kept,
    )
    recv = halo(faces)
    gathered, maps = call(
        scatter_kernel, [gathered_shape, Near((2 * owners, LANES))], to_owners(message),
        scratch=lists,
    )
    returned = coarse_solve(gathered, maps)
    direction, partial, message, *faces = call(
        direction_kernel,
        [vector, vector, message_shape] + halo_shapes(FACE, Far),
        returned, dof_order, traces, weights, local, *recv, loads, schur,
        far=[1, 4, 5, 10, 11], scratch=(one_hot,),
    )
    recv = halo(faces)
    received = to_owners(message)
    (gathered,) = call(
        scatter_both_kernel, [gathered_shape], received, maps, scratch=lists
    )
    local, *faces = call(
        image_kernel,
        [vector] + halo_shapes(FACE, Far),
        received, dof_order, weights, partial, *recv, neumann,
        far=[1, 3, 4, 9], scratch=(one_hot,),
    )
    recv = halo(faces)
    returned = coarse_solve(gathered, maps)
    search, scalars, message = call(
        last_kernel,
        [vector, small, message_shape],
        returned, dof_order, traces, weights, local, *recv, direction, loads, schur,
        far=[1, 4, 5, 10, 11, 12], scratch=(one_hot,),
    )
    (sums,) = call(sum_kernel, [Near((n_z * TILE, LANES))], to_owners(message))
    (out,) = call(
        finish_kernel, [vector], along_z(sums), scalars, direction, search, far=(2, 3)
    )
    return out


def solution(mesh):
    in_specs = (
        P(AXES, None, None),
        P(AXES, None, None),
        P(AXES, None, None),
        P(AXES, None, None),
        P(AXES, None, None),
        P(AXES, None),
        P(),
        P("sub", None),
    )
    return jax.shard_map(
        body, mesh=mesh, in_specs=in_specs, out_specs=P(AXES, None, None), check_vma=False
    )
```
